128 devices in a mesh: grp: 4 (over y), seq: 32 (over x, z, core).
Axes of the slice: x: 4, y: 4, z: 4, core: 2. Of those that a mesh axis runs over, the one named last changes fastest.
Arguments:
- phonemes: bfloat16 [4, 1536, 1024], P('grp', 'seq'), may hold values from -7 to 7
- durations: int32 [4, 1536], P('grp', 'seq'), may hold values from 1 to 673, as said below
- weights: bfloat16 [4, 1024, 1024], replicated, may hold values from -1 to 1
- d_out: bfloat16 [4, 12288, 1024], P('grp', 'seq'), may hold values from -6 to 6
Outputs:
- d_phonemes: bfloat16 [4, 1536, 1024], P('grp', 'seq')
- d_weights: float32 [4, 1024, 1024], P(None, ('grp', 'seq'))
The draws below stay inside these ranges and needn't reach their ends.
Inputs may be any that keep to these rules, and one draw needn't show every extreme that they name: In each chapter the durations sum to 12288, and the frames of the 48 phonemes at positions k * 48 to (k + 1) * 48 - 1 lie within frames (k - 1) * 384 to (k + 2) * 384 - 1; in every chapter some such block of phonemes reaches into both of these neighbouring frame ranges, and some phoneme lasts the largest duration.
All inputs are finite; a program needn't handle non-finite values.
Results may differ from the reference program's by a relative error of at most 0.018.
Values may be sent and summed in bfloat16 or wider, within the bound.
A program may use at most 128 MiB of HBM per device.

```python
import math
import jax
import jax.numpy as jnp
from jax import lax

D = 1024
HEADS = 16
WINDOW = 512
F_DEV = 384
P_DEV = 48
CHAPTERS = 4
PHONEMES = 1536
FRAMES = 12288


def draw_durations(key, part):
    key = jax.random.fold_in(key, 7)
    key_off, key_pick, key_share, key_pause = jax.random.split(key, 4)
    shards = PHONEMES // P_DEV
    spill_max = F_DEV * 7 // 16
    offsets = jax.random.randint(key_off, (CHAPTERS, shards + 1), -spill_max, spill_max + 1)
    chosen = jax.random.randint(key_pick, (CHAPTERS, 1), 1, shards - 1)
    columns = jnp.arange(shards + 1, dtype=jnp.int32)[None, :]
    offsets = jnp.where(columns == chosen, -spill_max, offsets)
    offsets = jnp.where(columns == chosen + 1, spill_max, offsets)
    offsets = jnp.where((columns == 0) | (columns == shards), 0, offsets)
    totals = F_DEV + offsets[:, 1:] - offsets[:, :-1]
    surplus = totals - P_DEV
    drawn = jax.random.randint(key_share, (CHAPTERS, shards, P_DEV), 1, 9)
    shares = drawn * drawn * drawn
    pause_at = jax.random.randint(key_pause, (CHAPTERS, 1, 1), 0, P_DEV)
    shard_ids = jnp.arange(shards, dtype=jnp.int32)[None, :, None]
    phon_ids = jnp.arange(P_DEV, dtype=jnp.int32)[None, None, :]
    single = (phon_ids == pause_at).astype(jnp.int32)
    shares = jnp.where(shard_ids == chosen[:, :, None], single, shares)
    running = jnp.cumsum(shares, axis=2)
    cut_marks = surplus[:, :, None] * running // running[:, :, -1:]
    previous = jnp.concatenate([jnp.zeros_like(cut_marks[:, :, :1]), cut_marks[:, :, :-1]], axis=2)
    return (1 + cut_marks - previous).reshape(CHAPTERS, PHONEMES).astype(jnp.int32)


def draw_phonemes(key, part):
    key = jax.random.fold_in(key, 13)
    key_val = jax.random.fold_in(key, 0)
    full_shape = (CHAPTERS, PHONEMES, D)
    return jnp.clip(jax.random.normal(key_val, full_shape, jnp.float32), -6.0, 6.0).astype(jnp.bfloat16)


def draw_weights(key, part):
    key = jax.random.fold_in(key, 17)
    key_main = jax.random.fold_in(key, 0)
    fan_scale = D ** (-0.5)
    drawn_all = jnp.clip(jax.random.normal(key_main, (4, D, D), jnp.float32), -4.5, 4.5) * fan_scale
    return drawn_all.astype(jnp.bfloat16)


def shard_levels(own_key, extent, cuts, smallest, top_value):
    factor_of = 1.0
    for position, shards_of in cuts:
        draws = jax.random.uniform(jax.random.fold_in(jax.random.fold_in(own_key, 6), position), (shards_of,), jnp.float32, smallest / len(cuts), top_value / len(cuts))
        factor_of = factor_of * jnp.repeat(jnp.exp(draws), extent[position] // shards_of).reshape((-1,) + (1,) * (len(extent) - 1 - position))
    return factor_of


def gaussian(key, dims, width, most, pieces=(), held_as=jnp.bfloat16):
    level = shard_levels(key, dims, pieces, -0.22, 0.18) if pieces else 1.0
    entries = jax.random.normal(key, dims, jnp.float32) * width * level
    return jnp.minimum(jnp.maximum(entries, -most), most).astype(held_as)


def setup_inputs(seed: int = 0) -> dict:
    key_of = jax.random.split(jax.random.key(seed), 5)
    phonemes = draw_phonemes(jax.random.fold_in(key_of[4], 71), 0)
    durations = draw_durations(jax.random.fold_in(key_of[4], 71), 0)
    weights = draw_weights(jax.random.fold_in(key_of[4], 71), 0)
    d_out = gaussian(key_of[3], (CHAPTERS, FRAMES, D), 1.0, 6.0, ((0, 4), (1, 32)))
    return dict(phonemes=phonemes, durations=durations, weights=weights, d_out=d_out)


def position_table(first_frame, frame_count, model_width):
    frame_ids = (first_frame + jnp.arange(frame_count, dtype=jnp.int32)).astype(jnp.float32)
    half_width = model_width // 2
    rates = jnp.exp(jnp.arange(half_width, dtype=jnp.float32) * (-math.log(10000.0) / half_width))
    angles = frame_ids[:, None] * rates[None, :]
    return jnp.concatenate([jnp.sin(angles), jnp.cos(angles)], axis=1)

def split_heads(matrix, head_count):
    return matrix.reshape(matrix.shape[0], head_count, matrix.shape[1] // head_count).transpose(1, 0, 2)

def merge_heads(stacked):
    return stacked.transpose(1, 0, 2).reshape(stacked.shape[1], stacked.shape[0] * stacked.shape[2])

def window_mask(first_query, first_key, query_rows, key_rows, frames_all, window_size):
    query_pos = first_query + jnp.arange(query_rows, dtype=jnp.int32)[:, None]
    key_pos = first_key + jnp.arange(key_rows, dtype=jnp.int32)[None, :]
    offset = key_pos - query_pos
    half_window = window_size // 2
    return (offset >= -half_window) & (offset < half_window) & (key_pos >= 0) & (key_pos < frames_all)

def probabilities(head_q, head_k, allowed):
    score_scale = head_q.shape[1] ** (-0.5)
    scores = jnp.dot(head_q, head_k.T, preferred_element_type=jnp.float32) * score_scale
    scores = jnp.where(allowed, scores, -jnp.inf)
    row_max = lax.optimization_barrier(jnp.max(scores, axis=1, keepdims=True))
    exp_scores = jnp.exp(scores - row_max)
    return exp_scores / lax.optimization_barrier(jnp.sum(exp_scores, axis=1, keepdims=True))

def forward_block(query, keyvals, allowed, head_count):
    model_width = query.shape[1]
    heads_q = split_heads(query, head_count)
    heads_k = split_heads(keyvals[:, :model_width], head_count)
    heads_v = split_heads(keyvals[:, model_width:], head_count)

    def one_head(head_item):
        head_q, head_k, head_v = head_item
        attn_probs = probabilities(head_q, head_k, allowed).astype(jnp.bfloat16)
        return jnp.dot(attn_probs, head_v, preferred_element_type=jnp.float32)
    return merge_heads(lax.map(one_head, (heads_q, heads_k, heads_v))).astype(jnp.bfloat16)

def backward_block(query, keyvals, d_attended, allowed, head_count):
    model_width = query.shape[1]
    heads_q = split_heads(query, head_count)
    heads_k = split_heads(keyvals[:, :model_width], head_count)
    heads_v = split_heads(keyvals[:, model_width:], head_count)
    heads_g = split_heads(d_attended, head_count)
    score_scale = heads_q.shape[2] ** (-0.5)

    def one_head(head_item):
        head_q, head_k, head_v, head_g = head_item
        attn_probs = probabilities(head_q, head_k, allowed)
        probs_low = attn_probs.astype(jnp.bfloat16)
        d_probs = jnp.dot(head_g, head_v.T, preferred_element_type=jnp.float32)
        d_values = jnp.dot(probs_low.T, head_g, preferred_element_type=jnp.float32)
        d_scores = attn_probs * (d_probs - lax.optimization_barrier(jnp.sum(attn_probs * d_probs, axis=1, keepdims=True)))
        d_low = (d_scores * score_scale).astype(jnp.bfloat16)
        d_query = jnp.dot(d_low, head_k, preferred_element_type=jnp.float32)
        d_keys = jnp.dot(d_low.T, head_q, preferred_element_type=jnp.float32)
        return (d_query, d_keys, d_values)
    d_query, d_keys, d_values = lax.map(one_head, (heads_q, heads_k, heads_v, heads_g))
    return (merge_heads(d_query), jnp.concatenate([merge_heads(d_keys), merge_heads(d_values)], axis=1))

def norm_backward(resid, cotan_low):
    row_mean = lax.optimization_barrier(jnp.mean(resid, axis=1, keepdims=True))
    centered = resid - row_mean
    inv_std = lax.rsqrt(lax.optimization_barrier(jnp.mean(centered * centered, axis=1, keepdims=True)) + 1e-05)
    normed = centered * inv_std
    cotan = cotan_low.astype(jnp.float32)
    return inv_std * (cotan - lax.optimization_barrier(jnp.mean(cotan, axis=1, keepdims=True)) - normed * lax.optimization_barrier(jnp.mean(cotan * normed, axis=1, keepdims=True)))

def reference(phonemes, durations, weights, d_out):
    chapter_count, frames_all, model_width = d_out.shape
    phon_count = phonemes.shape[1]
    query_rows = min(F_DEV, WINDOW)
    half_window = WINDOW // 2
    block_count = frames_all // query_rows
    w_query, w_key, w_value, w_out = (weights[0], weights[1], weights[2], weights[3])
    grad_terms = jnp.zeros((4, model_width, model_width), jnp.float32)
    results = []
    for chapter in range(chapter_count):
        phon_ends = jnp.cumsum(durations[chapter]).astype(jnp.int32)
        frame_ids = jnp.arange(frames_all, dtype=jnp.int32)
        frame_owner = jnp.searchsorted(phon_ends, frame_ids, side='right').astype(jnp.int32)
        expanded = jnp.take(phonemes[chapter], frame_owner, axis=0).astype(jnp.float32)
        inputs = (expanded + position_table(0, frames_all, model_width)).astype(jnp.bfloat16)
        query = jnp.dot(inputs, w_query, preferred_element_type=jnp.float32).astype(jnp.bfloat16)
        keys_all = jnp.dot(inputs, w_key, preferred_element_type=jnp.float32).astype(jnp.bfloat16)
        values_all = jnp.dot(inputs, w_value, preferred_element_type=jnp.float32).astype(jnp.bfloat16)
        padded = jnp.pad(jnp.concatenate([keys_all, values_all], axis=1), ((half_window, half_window), (0, 0)))

        def forward_one(block_index):
            row_start = block_index * query_rows
            query_block = lax.dynamic_slice_in_dim(query, row_start, query_rows, 0)
            keyval_block = lax.dynamic_slice_in_dim(padded, row_start, query_rows + WINDOW, 0)
            allowed = window_mask(row_start, row_start - half_window, query_rows, query_rows + WINDOW, frames_all, WINDOW)
            return forward_block(query_block, keyval_block, allowed, HEADS)
        block_ids = jnp.arange(block_count, dtype=jnp.int32)
        attended = lax.map(forward_one, block_ids).reshape(frames_all, model_width)
        resid = inputs.astype(jnp.float32) + jnp.dot(attended, w_out, preferred_element_type=jnp.float32)
        d_resid = norm_backward(resid, d_out[chapter])
        d_proj = d_resid.astype(jnp.bfloat16)
        d_attended = jnp.dot(d_proj, w_out.T, preferred_element_type=jnp.float32).astype(jnp.bfloat16)

        def backward_one(carried, block_index):
            row_start = block_index * query_rows
            query_block = lax.dynamic_slice_in_dim(query, row_start, query_rows, 0)
            keyval_block = lax.dynamic_slice_in_dim(padded, row_start, query_rows + WINDOW, 0)
            grad_block = lax.dynamic_slice_in_dim(d_attended, row_start, query_rows, 0)
            allowed = window_mask(row_start, row_start - half_window, query_rows, query_rows + WINDOW, frames_all, WINDOW)
            d_query, d_keyvals = backward_block(query_block, keyval_block, grad_block, allowed, HEADS)
            existing = lax.dynamic_slice_in_dim(carried, row_start, query_rows + WINDOW, 0)
            carried = lax.dynamic_update_slice_in_dim(carried, existing + d_keyvals, row_start, 0)
            return (carried, d_query)
        d_padded, d_query = lax.scan(backward_one, jnp.zeros((frames_all + WINDOW, 2 * model_width), jnp.float32), block_ids)
        d_query = d_query.reshape(frames_all, model_width).astype(jnp.bfloat16)
        d_keyvals = d_padded[half_window:half_window + frames_all]
        d_keys = d_keyvals[:, :model_width].astype(jnp.bfloat16)
        d_values = d_keyvals[:, model_width:].astype(jnp.bfloat16)
        grad_terms = grad_terms + jnp.stack([jnp.dot(inputs.T, d_query, preferred_element_type=jnp.float32), jnp.dot(inputs.T, d_keys, preferred_element_type=jnp.float32), jnp.dot(inputs.T, d_values, preferred_element_type=jnp.float32), jnp.dot(attended.T, d_proj, preferred_element_type=jnp.float32)])
        d_inputs = d_resid + jnp.dot(d_query, w_query.T, preferred_element_type=jnp.float32)
        d_inputs = d_inputs + jnp.dot(d_keys, w_key.T, preferred_element_type=jnp.float32)
        d_inputs = d_inputs + jnp.dot(d_values, w_value.T, preferred_element_type=jnp.float32)
        d_low = d_inputs.astype(jnp.bfloat16)
        d_phon = jax.ops.segment_sum(d_low.astype(jnp.float32), frame_owner, num_segments=phon_count)
        results.append(d_phon.astype(jnp.bfloat16))
    grad_scale = 1.0 / math.sqrt(chapter_count * frames_all)
    return (jnp.stack(results), grad_terms * grad_scale)
```

```python
import functools
import math

import jax
import jax.numpy as jnp
import numpy as np
from jax import lax
from jax.experimental import pallas as pl
from jax.experimental.pallas import tpu as pltpu
from jax.sharding import PartitionSpec as P

MESH = pl.DeviceIdType.MESH
BF16 = jnp.bfloat16
F32 = jnp.float32

D = 1024
HEADS = 16
WINDOW = 512
HALF = WINDOW // 2
F_DEV = 384
P_DEV = 48
SEQ = 32
GRP = 4
FRAMES = SEQ * F_DEV
EXT = F_DEV + WINDOW
TILE = 128
SPAN = TILE + WINDOW
TILES = F_DEV // TILE
PAIRS = HEADS // 2
NEAR = 5 * P_DEV
NEAR_PAD = 256
GROUPS = 4
COLS = D // GROUPS
GRAD_SCALE = 1.0 / math.sqrt(GRP * FRAMES)


def nn(a, b):
    return lax.dot_general(a, b, (((1,), (0,)), ((), ())), preferred_element_type=F32)


def nt(a, b):
    return lax.dot_general(a, b, (((1,), (1,)), ((), ())), preferred_element_type=F32)


def position_tables():
    half = D // 2
    rates = np.exp(np.arange(half) * (-math.log(10000.0) / half))
    tiles = SEQ * TILES + 2 * (HALF // TILE)
    coarse = (np.arange(tiles)[:, None] * TILE - HALF) * rates[None, :]
    fine = np.arange(TILE)[:, None] * rates[None, :]
    coarse = np.concatenate([np.sin(coarse), np.cos(coarse)], axis=1)
    fine = np.concatenate([np.sin(fine), np.cos(fine)], axis=1)
    pad = -coarse.shape[0] % 8
    coarse = np.pad(coarse, ((0, pad), (0, 0)))
    return coarse.astype(np.float32), fine.astype(np.float32)


def make_inputs(seq, near, bounds, coarse, fine, x, xt, oh, oht):
    half = D // 2
    begins = bounds[0:1, :]
    ends = bounds[1:2, :]

    @pl.loop(0, EXT // TILE)
    def _(i):
        rows = pl.ds(pl.multiple_of(i * TILE, TILE), TILE)
        frame = lax.broadcasted_iota(jnp.int32, (TILE, NEAR_PAD), 0) + (seq * F_DEV - HALF + i * TILE)
        onehot = jnp.where((frame >= begins) & (frame < ends), 1.0, 0.0)
        onehot_low = onehot.astype(BF16)
        oh[rows, :] = onehot_low
        expanded = nn(onehot_low, near[...])
        base = coarse[pl.ds(seq * TILES + i, 1), :]
        sin_a, cos_a = base[:, :half], base[:, half:]
        sin_b, cos_b = fine[:, :half], fine[:, half:]
        x[rows, :half] = (expanded[:, :half] + (sin_a * cos_b + cos_a * sin_b)).astype(BF16)
        x[rows, half:] = (expanded[:, half:] + (cos_a * cos_b - sin_a * sin_b)).astype(BF16)

    for i in range(EXT // TILE):
        rows = pl.ds(i * TILE, TILE)
        xt[:, rows] = x[rows, :].T
        oht[:, rows] = oh[rows, :].T


def make_projections(x, w, q, k, v, kt, vt):
    @pl.loop(0, D // 256)
    def _(n):
        cols = pl.ds(pl.multiple_of(n * 256, 256), 256)
        q[:, cols] = (nn(x[HALF : HALF + F_DEV, :], w[0, :, cols]).astype(BF16) * 0.125).astype(BF16)
        keys = nn(x[...], w[1, :, cols]).astype(BF16)
        k[:, cols] = keys
        kt[cols, :] = keys.T
        values = nn(x[...], w[2, :, cols]).astype(BF16)
        v[:, cols] = values
        vt[cols, :] = values.T


def make_bias(seq, bias):
    for i in range(TILES):
        key = lax.broadcasted_iota(jnp.int32, (SPAN, 2 * TILE), 0)
        query = lax.broadcasted_iota(jnp.int32, (SPAN, 2 * TILE), 1) % TILE
        frame = key + (seq * F_DEV - HALF + i * TILE)
        allowed = (key >= query) & (key < query + WINDOW) & (frame >= 0) & (frame < FRAMES)
        bias[i] = jnp.where(allowed, 0.0, -jnp.inf)


def two_heads(rows):
    lane = lax.broadcasted_iota(jnp.int32, rows.shape, 1)
    zero = jnp.zeros_like(rows)
    first = jnp.where(lane < 64, rows, zero)
    second = jnp.where(lane < 64, zero, rows)
    return jnp.concatenate([first, second], axis=0)


def own_halves(both):
    return jnp.concatenate([both[:64, :TILE], both[64:, TILE:]], axis=0)


def forward_attention(q, k, vt, bias, p, att_t):
    @pl.loop(0, PAIRS)
    def _(pair):
        cols = pl.ds(pl.multiple_of(pair * 128, 128), 128)
        for i in range(TILES):
            span = pl.ds(i * TILE, SPAN)
            rows = pl.ds(i * TILE, TILE)
            scores = nt(k[span, cols], two_heads(q[rows, cols])) + bias[i]
            peak = jnp.max(scores, axis=0, keepdims=True)
            raised = jnp.exp(scores - peak)
            total = jnp.sum(raised, axis=0, keepdims=True)
            probs = (raised * (1.0 / total)).astype(BF16)
            p[pair * TILES + i] = probs
            att_t[cols, rows] = own_halves(nn(vt[cols, span], probs)).astype(BF16)


def output_backward(x, att_t, d_out, w, d_proj, d_att):
    for i in range(TILES):
        rows = pl.ds(i * TILE, TILE)
        att = att_t[:, rows].T
        resid = x[HALF + i * TILE : HALF + (i + 1) * TILE, :].astype(F32) + nn(att, w[3])
        mean = jnp.mean(resid, axis=1, keepdims=True)
        centered = resid - mean
        inv_std = lax.rsqrt(jnp.mean(centered * centered, axis=1, keepdims=True) + 1e-5)
        normed = centered * inv_std
        cotan = d_out[rows, :].astype(F32)
        d_resid = inv_std * (
            cotan
            - jnp.mean(cotan, axis=1, keepdims=True)
            - normed * jnp.mean(cotan * normed, axis=1, keepdims=True)
        )
        d_proj[rows, :] = d_resid.astype(BF16)

    @pl.loop(0, D // 256)
    def _(n):
        cols = pl.ds(pl.multiple_of(n * 256, 256), 256)
        d_att[:, cols] = nt(d_proj[...], w[3, cols, :]).astype(BF16)


def backward_pair(pair, q, k, v, kt, d_att, p, dq_t, dk, dv, dk_sum, dv_sum):
    cols = pl.ds(pl.multiple_of(pair * 128, 128), 128)
    dk_sum[...] = jnp.zeros_like(dk_sum)
    dv_sum[...] = jnp.zeros_like(dv_sum)
    for i in range(TILES):
        span = pl.ds(i * TILE, SPAN)
        rows = pl.ds(i * TILE, TILE)
        both_q = two_heads(q[rows, cols])
        both_g = two_heads(d_att[rows, cols])
        probs_low = p[pair * TILES + i]
        d_probs = nt(v[span, cols], both_g)
        probs = probs_low.astype(F32)
        weighted = probs * d_probs
        delta = jnp.sum(weighted, axis=0, keepdims=True)
        d_low = (weighted - probs * delta).astype(BF16)
        dv_sum[span, :] += nn(probs_low, both_g)
        dk_sum[span, :] += nn(d_low, both_q)
        dq_t[cols, rows] = (own_halves(nn(kt[cols, span], d_low)) * 0.125).astype(BF16)
    dk[:, cols] = dk_sum[...].astype(BF16)
    dv[:, cols] = dv_sum[...].astype(BF16)


def blocks_of(product):
    count = product.shape[0] // 8
    cells = product.reshape(count, 8, COLS)
    return jnp.concatenate([cells[:, :, :128], cells[:, :, 128:]], axis=1).astype(BF16)


def split_cores(blocks):
    pairs = blocks.reshape(blocks.shape[0] // 2, 2, 16, 128)
    return pairs[:, 0], pairs[:, 1]


def weight_grad(product_of, store):
    for t in range(D // 256):
        first, second = split_cores(blocks_of(product_of(pl.ds(t * 256, 256))))
        store(0, t, first.reshape(4, 4, 16, 128))
        store(1, t, second.reshape(4, 4, 16, 128))


AXES = ("y", "x", "z")
ROTATIONS = (("z", "x", "y"), ("x", "y", "z"), ("y", "z", "x"))


def place():
    y = lax.axis_index("grp")
    seq = lax.axis_index("seq")
    return {"y": y, "x": seq // 8, "z": (seq // 2) % 4, "core": seq % 2, "seq": seq}


def device_of(at):
    return (at["y"], at["x"] * 8 + at["z"] * 2 + at["core"])


def along(at, axis, steps):
    moved = dict(at)
    moved[axis] = (at[axis] + steps) % 4
    return moved


def at_axis(ref, dims, axis, index):
    where = tuple(index if dim == axis else slice(None) for dim in dims)
    return ref.at[where]


class Reduction:
    def __init__(self, at, parts, from_core, sums, landed, core_sems, send_sems, recv_sems, turns):
        self.at, self.parts, self.from_core = at, parts, from_core
        self.sums, self.landed = (parts.at[at["core"]],) + sums, landed
        self.core_sems, self.send_sems, self.recv_sems = core_sems, send_sems, recv_sems
        self.turns = turns

    def core_copy(self):
        sibling = dict(self.at)
        sibling["core"] = 1 - self.at["core"]
        return pltpu.make_async_remote_copy(
            src_ref=self.parts.at[sibling["core"]],
            dst_ref=self.from_core,
            send_sem=self.core_sems.at[0],
            recv_sem=self.core_sems.at[1],
            device_id=device_of(sibling),
            device_id_type=MESH,
        )

    def axis_copy(self, stage, m, steps):
        order = ROTATIONS[self.turns[m]]
        axis = order[stage]
        dims = [dim for dim in AXES if dim not in order[:stage]]
        target = along(self.at, axis, steps)
        return pltpu.make_async_remote_copy(
            src_ref=at_axis(self.sums[stage].at[m], dims, axis, target[axis]),
            dst_ref=self.landed[stage].at[steps - 1, m],
            send_sem=self.send_sems.at[stage, m, steps - 1],
            recv_sem=self.recv_sems.at[stage, m, steps - 1],
            device_id=device_of(target),
            device_id_type=MESH,
        )

    def send_core(self):
        self.core_copy().start()

    def send_axis(self, stage):
        for m in range(len(self.turns)):
            for steps in (2, 1, 3):
                self.axis_copy(stage, m, steps).start()

    def first_sum(self):
        self.core_copy().wait_recv()
        for m in range(len(self.turns)):
            for y in range(4):
                total = self.sums[0][m, y].astype(F32) + self.from_core[m, y].astype(F32)
                self.sums[0][m, y] = total.astype(BF16)
        self.send_axis(0)

    def axis_total(self, stage, m):
        order = ROTATIONS[self.turns[m]]
        axis = order[stage]
        dims = [dim for dim in AXES if dim not in order[:stage]]
        for steps in (1, 3, 2):
            self.axis_copy(stage, m, steps).wait_recv()
        total = at_axis(self.sums[stage].at[m], dims, axis, self.at[axis])[...].astype(F32)
        for steps in (1, 2, 3):
            total = total + self.landed[stage][steps - 1, m].astype(F32)
        return total

    def next_sum(self, stage):
        for m in range(len(self.turns)):
            self.sums[stage][m] = self.axis_total(stage - 1, m).astype(BF16)
        self.send_axis(stage)

    def last_sum(self, put):
        for m in range(len(self.turns)):
            put(m, self.axis_total(2, m) * GRAD_SCALE)

    def drain(self):
        self.core_copy().wait_send()
        for stage in range(3):
            for m in range(len(self.turns)):
                for steps in (1, 2, 3):
                    self.axis_copy(stage, m, steps).wait_send()


def reduction_scratch(lead, n):
    return [
        pltpu.VMEM(lead + (2, n, 4, 4, 4, 16, 128), BF16),
        pltpu.VMEM(lead + (n, 4, 4, 4, 16, 128), BF16),
        pltpu.VMEM(lead + (n, 4, 4, 16, 128), BF16),
        pltpu.VMEM(lead + (n, 4, 16, 128), BF16),
        pltpu.VMEM(lead + (3, n, 4, 4, 16, 128), BF16),
        pltpu.VMEM(lead + (3, n, 4, 16, 128), BF16),
        pltpu.VMEM(lead + (3, n, 16, 128), BF16),
        pltpu.SemaphoreType.DMA(lead + (2,)),
        pltpu.SemaphoreType.DMA(lead + (3, n, 3)),
        pltpu.SemaphoreType.DMA(lead + (3, n, 3)),
    ]


def reduction_of(at, refs, turns):
    parts, from_core, s1, s2, l0, l1, l2, core_sems, send_sems, recv_sems = refs
    return Reduction(
        at, parts, from_core, (s1, s2), (l0, l1, l2), core_sems, send_sems, recv_sems, turns
    )


def greet(at):
    barrier = pltpu.get_barrier_semaphore()

    @pl.loop(1, SEQ)
    def _(steps):
        pl.semaphore_signal(
            barrier,
            inc=1,
            device_id=(at["y"], (at["seq"] + steps) % SEQ),
            device_id_type=MESH,
        )

    for steps in (1, 2, 3):
        pl.semaphore_signal(
            barrier, inc=1, device_id=device_of(along(at, "y", steps)), device_id_type=MESH
        )
    pl.semaphore_wait(barrier, SEQ - 1 + 3)


NEAR_STEPS = (1, -1, 2, -2)


def near_copy(at, phonemes, near, sems, i):
    steps = NEAR_STEPS[i]
    return pltpu.make_async_remote_copy(
        src_ref=phonemes.at[0],
        dst_ref=near.at[pl.ds((2 - steps) * P_DEV, P_DEV)],
        send_sem=sems.at[0, i],
        recv_sem=sems.at[1, i],
        device_id=(at["y"], (at["seq"] + steps + SEQ) % SEQ),
        device_id_type=MESH,
    )


def duration_copy(at, own, all_durations, sems, steps):
    return pltpu.make_async_remote_copy(
        src_ref=own,
        dst_ref=all_durations.at[at["seq"]],
        send_sem=sems.at[0],
        recv_sem=sems.at[1],
        device_id=(at["y"], (at["seq"] + steps) % SEQ),
        device_id_type=MESH,
    )


def make_bounds(seq, all_durations, rows, bounds):
    everyone = all_durations[:, 0, :]
    block_of = lax.broadcasted_iota(jnp.int32, (SEQ, 128), 0)
    rows[...] = jnp.zeros_like(rows)
    before = []
    for i in range(5):
        index = (seq + i - 2 + SEQ) % SEQ
        rows[i : i + 1, :] = all_durations[index][0:1, :]
        earlier = jnp.sum(jnp.where(block_of < index, everyone, 0), axis=0, keepdims=True)
        before.append(jnp.sum(earlier, axis=1, keepdims=True))
    lane = lax.broadcasted_iota(jnp.int32, (8, 128), 1)
    lengths = rows[...]
    running = lengths
    for shift in (1, 2, 4, 8, 16, 32):
        running = running + jnp.where(lane >= shift, pltpu.roll(running, shift, 1), 0)
    valid = lane < P_DEV
    ends = jnp.where(valid, running, 0)
    begins = jnp.where(valid, running - lengths, 0)
    empty = jnp.zeros((8, 128), jnp.int32)
    all_ends = jnp.zeros((1, 256), jnp.int32)
    all_begins = jnp.zeros((1, 256), jnp.int32)
    wide = lax.broadcasted_iota(jnp.int32, (1, 256), 1)
    for i in range(5):
        here = (wide >= i * P_DEV) & (wide < (i + 1) * P_DEV)
        end_row = jnp.concatenate([ends, empty], axis=1)
        begin_row = jnp.concatenate([begins, empty], axis=1)
        if i:
            end_row = pltpu.roll(end_row, i * P_DEV, 1)
            begin_row = pltpu.roll(begin_row, i * P_DEV, 1)
        all_ends = jnp.where(here, end_row[i : i + 1] + before[i], all_ends)
        all_begins = jnp.where(here, begin_row[i : i + 1] + before[i], all_begins)
    bounds[0:1, :] = all_begins
    bounds[1:2, :] = all_ends


def sum_copy(at, near_sums, landed, sems, i):
    steps = NEAR_STEPS[i]
    return pltpu.make_async_remote_copy(
        src_ref=near_sums.at[pl.ds((2 + steps) * P_DEV, P_DEV)],
        dst_ref=landed.at[i],
        send_sem=sems.at[0, i],
        recv_sem=sems.at[1, i],
        device_id=(at["y"], (at["seq"] + steps + SEQ) % SEQ),
        device_id_type=MESH,
    )


def phoneme_sums(oht, dq_t, dk, dv, d_proj, w, low_q, low_k, low_v, near_sums):
    own = pl.ds(HALF, F_DEV)

    @pl.loop(0, D // 256)
    def _(n):
        cols = pl.ds(pl.multiple_of(n * 256, 256), 256)
        low_q[:, cols] = nt(oht[:, own], dq_t[cols, :]).astype(BF16)
        low_k[:, cols] = nn(oht[...], dk[:, cols]).astype(BF16)
        low_v[:, cols] = nn(oht[...], dv[:, cols]).astype(BF16)

    @pl.loop(0, D // 256)
    def _(n):
        cols = pl.ds(pl.multiple_of(n * 256, 256), 256)
        total = nn(oht[:, own], d_proj[:, cols])
        total = total + nt(low_q[...], w[0, cols, :])
        total = total + nt(low_k[...], w[1, cols, :])
        total = total + nt(low_v[...], w[2, cols, :])
        near_sums[:, cols] = total.astype(BF16)


def kernel(
    phonemes, durations, weights, d_out, coarse, fine, d_phon, d_weights, *scratch
):
    (
        w, cotan, dur_own, dur_all, dur_rows, bounds, near, x, xt, oh, oht, q, k, v, kt, vt,
        bias, p, att_t, d_proj, d_att, dq_t, dk, dv, dk_sum, dv_sum, sums_landed, load_sems, dur_sems, near_sems, sum_sems, *rest
    ) = scratch
    out_refs, qkv_refs = rest[: len(rest) // 2], rest[len(rest) // 2 :]
    at = place()
    seq = at["seq"]

    loads = [pltpu.make_async_copy(weights.at[m], w.at[m], load_sems.at[m]) for m in range(4)]
    loads.append(pltpu.make_async_copy(d_out.at[0], cotan, load_sems.at[4]))
    for load in loads:
        load.start()

    dur_own[...] = jnp.zeros_like(dur_own)
    dur_own[0:1, 0:P_DEV] = durations[...]
    dur_all[seq] = dur_own[...]
    near[2 * P_DEV : 3 * P_DEV, :] = phonemes[0]
    near[NEAR:, :] = jnp.zeros((NEAR_PAD - NEAR, D), BF16)

    greet(at)

    @pl.loop(1, SEQ)
    def _(steps):
        duration_copy(at, dur_own, dur_all, dur_sems, steps).start()

    for i in range(4):
        near_copy(at, phonemes, near, near_sems, i).start()
    make_bias(seq, bias)

    others = dur_all.at[pl.ds(0, SEQ - 1)]
    pltpu.make_async_copy(others, others, dur_sems.at[1]).wait()
    make_bounds(seq, dur_all, dur_rows, bounds)
    for i in range(4):
        near_copy(at, phonemes, near, near_sems, i).wait_recv()

    make_inputs(seq, near, bounds, coarse, fine, x, xt, oh, oht)
    for m in range(3):
        loads[m].wait()
    make_projections(x, w, q, k, v, kt, vt)
    forward_attention(q, k, vt, bias, p, att_t)
    loads[3].wait()
    loads[4].wait()
    output_backward(x, att_t, cotan, w, d_proj, d_att)

    out_turn = reduction_of(at, out_refs, (0, 1, 2, 0))
    for j in range(GROUPS):
        cols = pl.ds(j * COLS, COLS)

        def store(core, block, value):
            out_refs[0][core, j, block] = value

        weight_grad(lambda rows: nn(att_t[rows, :], d_proj[:, cols]), store)
    out_turn.send_core()

    turns = [
        reduction_of(at, [ref.at[g] for ref in qkv_refs], (0, 1, 2)) for g in range(GROUPS)
    ]

    def put_out(m, total):
        cols = m * COLS
        d_weights[3, :, cols : cols + 128] = total[:8]
        d_weights[3, :, cols + 128 : cols + COLS] = total[8:]

    def steps_of(turn, put):
        return [
            turn.first_sum,
            lambda: turn.next_sum(1),
            lambda: turn.next_sum(2),
            lambda: turn.last_sum(put),
        ]

    def put_of(g):
        def put(m, total):
            cols = g * COLS
            d_weights[m, :, cols : cols + 128] = total[:8]
            d_weights[m, :, cols + 128 : cols + COLS] = total[8:]

        return put

    pending = steps_of(out_turn, put_out)
    for g in range(GROUPS):
        for half in range(2):
            backward_pair(
                g * 2 + half, q, k, v, kt, d_att, p, dq_t, dk, dv, dk_sum, dv_sum
            )
            for _ in range(2):
                if pending:
                    pending.pop(0)()
        cols = pl.ds(g * COLS, COLS)
        own = pl.ds(HALF, F_DEV)
        products = [
            lambda rows: nt(xt[rows, own], dq_t[cols, :]),
            lambda rows: nn(xt[rows, :], dk[:, cols]),
            lambda rows: nn(xt[rows, :], dv[:, cols]),
        ]
        for m in range(3):

            def store(core, block, value):
                qkv_refs[0][g, core, m, block] = value

            weight_grad(products[m], store)
        turns[g].send_core()
        pending = steps_of(turns[g], put_of(g))

    pending.pop(0)()
    near_sums = near
    low_q, low_k, low_v = [x.at[pl.ds(m * NEAR_PAD, NEAR_PAD)] for m in range(3)]
    phoneme_sums(oht, dq_t, dk, dv, d_proj, w, low_q, low_k, low_v, near_sums)
    for i in range(4):
        sum_copy(at, near_sums, sums_landed, sum_sems, i).start()
    for step in pending:
        step()
    total = near_sums[2 * P_DEV : 3 * P_DEV, :].astype(F32)
    for i in range(4):
        sum_copy(at, near_sums, sums_landed, sum_sems, i).wait_recv()
        total = total + sums_landed[i].astype(F32)
    d_phon[0] = total.astype(BF16)

    pltpu.make_async_copy(others, others, dur_sems.at[0]).wait()
    for i in range(4):
        near_copy(at, phonemes, near, near_sems, i).wait_send()
        sum_copy(at, near_sums, sums_landed, sum_sems, i).wait_send()
    out_turn.drain()
    for turn in turns:
        turn.drain()


def on_device(phonemes, durations, weights, d_out):
    coarse, fine = position_tables()
    vmem = pl.BlockSpec(memory_space=pltpu.VMEM)
    hbm = pl.BlockSpec(memory_space=pl.ANY)
    scratch = [
        pltpu.VMEM((4, D, D), BF16),
        pltpu.VMEM((F_DEV, D), BF16),
        pltpu.VMEM((8, 128), jnp.int32),
        pltpu.VMEM((SEQ, 8, 128), jnp.int32),
        pltpu.VMEM((8, 128), jnp.int32),
        pltpu.VMEM((8, NEAR_PAD), jnp.int32),
        pltpu.VMEM((NEAR_PAD, D), BF16),
        pltpu.VMEM((EXT, D), BF16),
        pltpu.VMEM((D, EXT), BF16),
        pltpu.VMEM((EXT, NEAR_PAD), BF16),
        pltpu.VMEM((NEAR_PAD, EXT), BF16),
        pltpu.VMEM((F_DEV, D), BF16),
        pltpu.VMEM((EXT, D), BF16),
        pltpu.VMEM((EXT, D), BF16),
        pltpu.VMEM((D, EXT), BF16),
        pltpu.VMEM((D, EXT), BF16),
        pltpu.VMEM((TILES, SPAN, 2 * TILE), F32),
        pltpu.VMEM((PAIRS * TILES, SPAN, 2 * TILE), BF16),
        pltpu.VMEM((D, F_DEV), BF16),
        pltpu.VMEM((F_DEV, D), BF16),
        pltpu.VMEM((F_DEV, D), BF16),
        pltpu.VMEM((D, F_DEV), BF16),
        pltpu.VMEM((EXT, D), BF16),
        pltpu.VMEM((EXT, D), BF16),
        pltpu.VMEM((EXT, 128), F32),
        pltpu.VMEM((EXT, 128), F32),
        pltpu.VMEM((4, P_DEV, D), BF16),
        pltpu.SemaphoreType.DMA((5,)),
        pltpu.SemaphoreType.DMA((2,)),
        pltpu.SemaphoreType.DMA((2, 4)),
        pltpu.SemaphoreType.DMA((2, 4)),
    ]
    scratch += reduction_scratch((), 4)
    scratch += reduction_scratch((GROUPS,), 3)
    return pl.pallas_call(
        kernel,
        out_shape=(
            jax.ShapeDtypeStruct((1, P_DEV, D), BF16),
            jax.ShapeDtypeStruct((4, 8, D), F32),
        ),
        in_specs=[vmem, vmem, hbm, hbm, vmem, vmem],
        out_specs=(vmem, vmem),
        scratch_shapes=scratch,
        compiler_params=pltpu.CompilerParams(
            collective_id=0, has_side_effects=True, vmem_limit_bytes=62 * 1024 * 1024
        ),
    )(phonemes, durations, weights, d_out, coarse, fine)


def solution(mesh):
    return jax.shard_map(
        on_device,
        mesh=mesh,
        in_specs=(P("grp", "seq", None), P("grp", "seq"), P(), P("grp", "seq", None)),
        out_specs=(P("grp", "seq", None), P(None, ("grp", "seq"), None)),
        check_vma=False,
    )
```

```python
import functools
import math

import jax
import jax.numpy as jnp
import numpy as np
from jax import lax
from jax.experimental import pallas as pl
from jax.experimental.pallas import tpu as pltpu
from jax.sharding import PartitionSpec as P

MESH = pl.DeviceIdType.MESH
BF16 = jnp.bfloat16
F32 = jnp.float32

D = 1024
HEADS = 16
WINDOW = 512
HALF = WINDOW // 2
F_DEV = 384
P_DEV = 48
SEQ = 32
GRP = 4
FRAMES = SEQ * F_DEV
EXT = F_DEV + WINDOW
TILE = 128
SPAN = TILE + WINDOW
TILES = F_DEV // TILE
PAIRS = HEADS // 2
NEAR = 5 * P_DEV
NEAR_PAD = 256
GROUPS = 4
COLS = D // GROUPS
GRAD_SCALE = 1.0 / math.sqrt(GRP * FRAMES)


def nn(a, b):
    return lax.dot_general(a, b, (((1,), (0,)), ((), ())), preferred_element_type=F32)


def nt(a, b):
    return lax.dot_general(a, b, (((1,), (1,)), ((), ())), preferred_element_type=F32)


def position_tables():
    half = D // 2
    rates = np.exp(np.arange(half) * (-math.log(10000.0) / half))
    tiles = SEQ * TILES + 2 * (HALF // TILE)
    coarse = (np.arange(tiles)[:, None] * TILE - HALF) * rates[None, :]
    fine = np.arange(TILE)[:, None] * rates[None, :]
    coarse = np.concatenate([np.sin(coarse), np.cos(coarse)], axis=1)
    fine = np.concatenate([np.sin(fine), np.cos(fine)], axis=1)
    pad = -coarse.shape[0] % 8
    coarse = np.pad(coarse, ((0, pad), (0, 0)))
    return coarse.astype(np.float32), fine.astype(np.float32)


def make_inputs(seq, near, bounds, coarse, fine, x, xt, oht):
    half = D // 2
    begins = bounds[0:1, :]
    ends = bounds[1:2, :]

    @pl.loop(0, EXT // TILE)
    def _(i):
        rows = pl.ds(pl.multiple_of(i * TILE, TILE), TILE)
        frame = lax.broadcasted_iota(jnp.int32, (TILE, NEAR_PAD), 0) + (seq * F_DEV - HALF + i * TILE)
        onehot = jnp.where((frame >= begins) & (frame < ends), 1.0, 0.0)
        onehot_low = onehot.astype(BF16)
        oht[:, rows] = onehot_low.T
        expanded = nn(onehot_low, near[...])
        base = coarse[pl.ds(seq * TILES + i, 1), :]
        sin_a, cos_a = base[:, :half], base[:, half:]
        sin_b, cos_b = fine[:, :half], fine[:, half:]
        x[rows, :half] = (expanded[:, :half] + (sin_a * cos_b + cos_a * sin_b)).astype(BF16)
        x[rows, half:] = (expanded[:, half:] + (cos_a * cos_b - sin_a * sin_b)).astype(BF16)

    for i in range(EXT // TILE):
        rows = pl.ds(i * TILE, TILE)
        xt[:, rows] = x[rows, :].T


def make_projections(x, w, q, k, v, kt, vt):
    @pl.loop(0, D // 256)
    def _(n):
        cols = pl.ds(pl.multiple_of(n * 256, 256), 256)
        q[:, cols] = (nn(x[HALF : HALF + F_DEV, :], w[0, :, cols]).astype(BF16) * 0.125).astype(BF16)
        keys = nn(x[...], w[1, :, cols]).astype(BF16)
        k[:, cols] = keys
        kt[cols, :] = keys.T
        values = nn(x[...], w[2, :, cols]).astype(BF16)
        v[:, cols] = values
        vt[cols, :] = values.T


def make_bias(seq, bias):
    for i in range(TILES):
        key = lax.broadcasted_iota(jnp.int32, (SPAN, 2 * TILE), 0)
        query = lax.broadcasted_iota(jnp.int32, (SPAN, 2 * TILE), 1) % TILE
        frame = key + (seq * F_DEV - HALF + i * TILE)
        allowed = (key >= query) & (key < query + WINDOW) & (frame >= 0) & (frame < FRAMES)
        bias[i] = jnp.where(allowed, 0.0, -jnp.inf)


def two_heads(rows):
    lane = lax.broadcasted_iota(jnp.int32, rows.shape, 1)
    zero = jnp.zeros_like(rows)
    first = jnp.where(lane < 64, rows, zero)
    second = jnp.where(lane < 64, zero, rows)
    return jnp.concatenate([first, second], axis=0)


def own_halves(both):
    return jnp.concatenate([both[:64, :TILE], both[64:, TILE:]], axis=0)


def forward_attention(q, k, vt, bias, p, att_t):
    def make_probs(pair):
        cols = pl.ds(pl.multiple_of(pair * 128, 128), 128)
        for i in range(TILES):
            span = pl.ds(i * TILE, SPAN)
            rows = pl.ds(i * TILE, TILE)
            scores = nt(k[span, cols], two_heads(q[rows, cols])) + bias[i]
            peak = jnp.max(scores, axis=0, keepdims=True)
            raised = jnp.exp(scores - peak)
            total = jnp.sum(raised, axis=0, keepdims=True)
            p[pair * TILES + i] = (raised * (1.0 / total)).astype(BF16)

    def attend(pair):
        cols = pl.ds(pl.multiple_of(pair * 128, 128), 128)
        for i in range(TILES):
            span = pl.ds(i * TILE, SPAN)
            rows = pl.ds(i * TILE, TILE)
            att_t[cols, rows] = own_halves(nn(vt[cols, span], p[pair * TILES + i])).astype(BF16)

    make_probs(0)

    @pl.loop(1, PAIRS)
    def _(pair):
        attend(pair - 1)
        make_probs(pair)

    attend(PAIRS - 1)


def output_backward(x, att_t, d_out, w, d_proj):
    for i in range(TILES):
        rows = pl.ds(i * TILE, TILE)
        att = att_t[:, rows].T
        resid = x[HALF + i * TILE : HALF + (i + 1) * TILE, :].astype(F32) + nn(att, w[3])
        mean = jnp.mean(resid, axis=1, keepdims=True)
        centered = resid - mean
        inv_std = lax.rsqrt(jnp.mean(centered * centered, axis=1, keepdims=True) + 1e-5)
        normed = centered * inv_std
        cotan = d_out[rows, :].astype(F32)
        d_resid = inv_std * (
            cotan
            - jnp.mean(cotan, axis=1, keepdims=True)
            - normed * jnp.mean(cotan * normed, axis=1, keepdims=True)
        )
        d_proj[rows, :] = d_resid.astype(BF16)


def attended_grads(w, d_proj, d_att):
    @pl.loop(0, D // 256)
    def _(n):
        cols = pl.ds(pl.multiple_of(n * 256, 256), 256)
        d_att[:, cols] = nt(d_proj[...], w[3, cols, :]).astype(BF16)


def score_grads(pair, v, d_att, p, ds):
    cols = pl.ds(pair * 128, 128)
    for i in range(TILES):
        both_g = two_heads(d_att[i * TILE : (i + 1) * TILE, cols])
        d_probs = nt(v[pl.ds(i * TILE, SPAN), cols], both_g)
        probs = p[pair * TILES + i].astype(F32)
        weighted = probs * d_probs
        delta = jnp.sum(weighted, axis=0, keepdims=True)
        ds[pair % 2, i] = (weighted - probs * delta).astype(BF16)


def key_sums(cells, rights, put):
    first, second, third = rights
    middle = jnp.concatenate([cells(0, 256, 640), cells(1, 128, 512), cells(2, 0, 384)], axis=1)
    put(256, nn(middle, jnp.concatenate([first, second, third], axis=0)))
    put(0, nn(cells(0, 0, 128), first))
    near = jnp.concatenate([cells(0, 128, 256), cells(1, 0, 128)], axis=1)
    put(128, nn(near, jnp.concatenate([first, second], axis=0)))
    far = jnp.concatenate([cells(1, 512, 640), cells(2, 384, 512)], axis=1)
    put(640, nn(far, jnp.concatenate([second, third], axis=0)))
    put(768, nn(cells(2, 512, 640), third))


def pair_grads(pair, q, kt, d_att, p, ds, dq_t, dk, dv):
    cols = pl.ds(pair * 128, 128)
    tiles = [pl.ds(i * TILE, TILE) for i in range(TILES)]

    def put_keys(row, value):
        dk[pl.ds(row, value.shape[0]), cols] = value.astype(BF16)

    def put_values(row, value):
        dv[pl.ds(row, value.shape[0]), cols] = value.astype(BF16)

    for i in range(TILES):
        both = nn(kt[cols, pl.ds(i * TILE, SPAN)], ds[pair % 2, i])
        dq_t[cols, tiles[i]] = (own_halves(both) * 0.125).astype(BF16)
    key_sums(
        lambda i, begin, end: ds[pair % 2, i, begin:end, :],
        [two_heads(q[rows, cols]) for rows in tiles],
        put_keys,
    )
    key_sums(
        lambda i, begin, end: p[pair * TILES + i, begin:end, :],
        [two_heads(d_att[rows, cols]) for rows in tiles],
        put_values,
    )


def blocks_of(product):
    count = product.shape[0] // 8
    cells = product.reshape(count, 8, COLS)
    return jnp.concatenate([cells[:, :, :128], cells[:, :, 128:]], axis=1).astype(BF16)


def split_cores(blocks):
    pairs = blocks.reshape(blocks.shape[0] // 2, 2, 16, 128)
    return pairs[:, 0], pairs[:, 1]


def weight_grad(product_of, store):
    for t in range(D // 256):
        first, second = split_cores(blocks_of(product_of(pl.ds(t * 256, 256))))
        store(0, t, first.reshape(4, 4, 16, 128))
        store(1, t, second.reshape(4, 4, 16, 128))


AXES = ("y", "x", "z")
ROTATIONS = (("z", "x", "y"), ("x", "y", "z"), ("y", "z", "x"))


def place():
    y = lax.axis_index("grp")
    seq = lax.axis_index("seq")
    return {"y": y, "x": seq // 8, "z": (seq // 2) % 4, "core": seq % 2, "seq": seq}


def device_of(at):
    return (at["y"], at["x"] * 8 + at["z"] * 2 + at["core"])


def along(at, axis, steps):
    moved = dict(at)
    moved[axis] = (at[axis] + steps) % 4
    return moved


def at_axis(ref, dims, axis, index):
    where = tuple(index if dim == axis else slice(None) for dim in dims)
    return ref.at[where]


class Reduction:
    def __init__(self, at, parts, from_core, sums, landed, core_sems, send_sems, recv_sems, turns):
        self.at, self.parts, self.from_core = at, parts, from_core
        self.sums, self.landed = (parts.at[at["core"]],) + sums, landed
        self.core_sems, self.send_sems, self.recv_sems = core_sems, send_sems, recv_sems
        self.turns = turns

    def core_copy(self):
        sibling = dict(self.at)
        sibling["core"] = 1 - self.at["core"]
        return pltpu.make_async_remote_copy(
            src_ref=self.parts.at[sibling["core"]],
            dst_ref=self.from_core,
            send_sem=self.core_sems.at[0],
            recv_sem=self.core_sems.at[1],
            device_id=device_of(sibling),
            device_id_type=MESH,
        )

    def axis_copy(self, stage, m, steps):
        order = ROTATIONS[self.turns[m]]
        axis = order[stage]
        dims = [dim for dim in AXES if dim not in order[:stage]]
        target = along(self.at, axis, steps)
        return pltpu.make_async_remote_copy(
            src_ref=at_axis(self.sums[stage].at[m], dims, axis, target[axis]),
            dst_ref=self.landed[stage].at[steps - 1, m],
            send_sem=self.send_sems.at[stage, m, steps - 1],
            recv_sem=self.recv_sems.at[stage, m, steps - 1],
            device_id=device_of(target),
            device_id_type=MESH,
        )

    def send_core(self):
        self.core_copy().start()

    def send_axis(self, stage):
        for m in range(len(self.turns)):
            for steps in (2, 1, 3):
                self.axis_copy(stage, m, steps).start()

    def first_sum(self):
        self.core_copy().wait_recv()
        for m in range(len(self.turns)):
            for y in range(4):
                total = self.sums[0][m, y].astype(F32) + self.from_core[m, y].astype(F32)
                self.sums[0][m, y] = total.astype(BF16)
        self.send_axis(0)

    def axis_total(self, stage, m):
        order = ROTATIONS[self.turns[m]]
        axis = order[stage]
        dims = [dim for dim in AXES if dim not in order[:stage]]
        for steps in (1, 3, 2):
            self.axis_copy(stage, m, steps).wait_recv()
        total = at_axis(self.sums[stage].at[m], dims, axis, self.at[axis])[...].astype(F32)
        for steps in (1, 2, 3):
            total = total + self.landed[stage][steps - 1, m].astype(F32)
        return total

    def next_sum(self, stage):
        for m in range(len(self.turns)):
            self.sums[stage][m] = self.axis_total(stage - 1, m).astype(BF16)
        self.send_axis(stage)

    def last_sum(self, put):
        for m in range(len(self.turns)):
            put(m, self.axis_total(2, m) * GRAD_SCALE)

    def drain(self):
        self.core_copy().wait_send()
        for stage in range(3):
            for m in range(len(self.turns)):
                for steps in (1, 2, 3):
                    self.axis_copy(stage, m, steps).wait_send()


def reduction_scratch(lead, n):
    return [
        pltpu.VMEM(lead + (2, n, 4, 4, 4, 16, 128), BF16),
        pltpu.VMEM(lead + (n, 4, 4, 4, 16, 128), BF16),
        pltpu.VMEM(lead + (n, 4, 4, 16, 128), BF16),
        pltpu.VMEM(lead + (n, 4, 16, 128), BF16),
        pltpu.VMEM(lead + (3, n, 4, 4, 16, 128), BF16),
        pltpu.VMEM(lead + (3, n, 4, 16, 128), BF16),
        pltpu.VMEM(lead + (3, n, 16, 128), BF16),
        pltpu.SemaphoreType.DMA(lead + (2,)),
        pltpu.SemaphoreType.DMA(lead + (3, n, 3)),
        pltpu.SemaphoreType.DMA(lead + (3, n, 3)),
    ]


def reduction_of(at, refs, turns):
    parts, from_core, s1, s2, l0, l1, l2, core_sems, send_sems, recv_sems = refs
    return Reduction(
        at, parts, from_core, (s1, s2), (l0, l1, l2), core_sems, send_sems, recv_sems, turns
    )


def greet(at):
    barrier = pltpu.get_barrier_semaphore()

    @pl.loop(1, SEQ)
    def _(steps):
        pl.semaphore_signal(
            barrier,
            inc=1,
            device_id=(at["y"], (at["seq"] + steps) % SEQ),
            device_id_type=MESH,
        )

    for steps in (1, 2, 3):
        pl.semaphore_signal(
            barrier, inc=1, device_id=device_of(along(at, "y", steps)), device_id_type=MESH
        )


def await_greetings():
    pl.semaphore_wait(pltpu.get_barrier_semaphore(), SEQ - 1 + 3)


NEAR_STEPS = (1, -1, 2, -2)


def near_copy(at, phonemes, near, sems, i):
    steps = NEAR_STEPS[i]
    return pltpu.make_async_remote_copy(
        src_ref=phonemes.at[0],
        dst_ref=near.at[pl.ds((2 - steps) * P_DEV, P_DEV)],
        send_sem=sems.at[0, i],
        recv_sem=sems.at[1, i],
        device_id=(at["y"], (at["seq"] + steps + SEQ) % SEQ),
        device_id_type=MESH,
    )


def duration_copy(at, own, all_durations, sems, steps):
    return pltpu.make_async_remote_copy(
        src_ref=own,
        dst_ref=all_durations.at[at["seq"]],
        send_sem=sems.at[0],
        recv_sem=sems.at[1],
        device_id=(at["y"], (at["seq"] + steps) % SEQ),
        device_id_type=MESH,
    )


def make_bounds(seq, all_durations, rows, bounds):
    everyone = all_durations[:, 0, :]
    block_of = lax.broadcasted_iota(jnp.int32, (SEQ, 128), 0)
    rows[...] = jnp.zeros_like(rows)
    before = []
    for i in range(5):
        index = (seq + i - 2 + SEQ) % SEQ
        rows[i : i + 1, :] = all_durations[index][0:1, :]
        earlier = jnp.sum(jnp.where(block_of < index, everyone, 0), axis=0, keepdims=True)
        before.append(jnp.sum(earlier, axis=1, keepdims=True))
    lane = lax.broadcasted_iota(jnp.int32, (8, 128), 1)
    lengths = rows[...]
    running = lengths
    for shift in (1, 2, 4, 8, 16, 32):
        running = running + jnp.where(lane >= shift, pltpu.roll(running, shift, 1), 0)
    valid = lane < P_DEV
    ends = jnp.where(valid, running, 0)
    begins = jnp.where(valid, running - lengths, 0)
    empty = jnp.zeros((8, 128), jnp.int32)
    all_ends = jnp.zeros((1, 256), jnp.int32)
    all_begins = jnp.zeros((1, 256), jnp.int32)
    wide = lax.broadcasted_iota(jnp.int32, (1, 256), 1)
    for i in range(5):
        here = (wide >= i * P_DEV) & (wide < (i + 1) * P_DEV)
        end_row = jnp.concatenate([ends, empty], axis=1)
        begin_row = jnp.concatenate([begins, empty], axis=1)
        if i:
            end_row = pltpu.roll(end_row, i * P_DEV, 1)
            begin_row = pltpu.roll(begin_row, i * P_DEV, 1)
        all_ends = jnp.where(here, end_row[i : i + 1] + before[i], all_ends)
        all_begins = jnp.where(here, begin_row[i : i + 1] + before[i], all_begins)
    bounds[0:1, :] = all_begins
    bounds[1:2, :] = all_ends


def sum_copy(at, near_sums, landed, sems, i):
    steps = NEAR_STEPS[i]
    return pltpu.make_async_remote_copy(
        src_ref=near_sums.at[pl.ds((2 + steps) * P_DEV, P_DEV)],
        dst_ref=landed.at[i],
        send_sem=sems.at[0, i],
        recv_sem=sems.at[1, i],
        device_id=(at["y"], (at["seq"] + steps + SEQ) % SEQ),
        device_id_type=MESH,
    )


def phoneme_low(oht, dq_t, dk, dv, low_q, low_k, low_v):
    own = pl.ds(HALF, F_DEV)

    @pl.loop(0, D // 256)
    def _(n):
        cols = pl.ds(pl.multiple_of(n * 256, 256), 256)
        low_q[:, cols] = nt(oht[:, own], dq_t[cols, :]).astype(BF16)
        low_k[:, cols] = nn(oht[...], dk[:, cols]).astype(BF16)
        low_v[:, cols] = nn(oht[...], dv[:, cols]).astype(BF16)


def phoneme_sums(oht, d_proj, w, low_q, low_k, low_v, near_sums):
    own = pl.ds(HALF, F_DEV)

    @pl.loop(0, D // 256)
    def _(n):
        cols = pl.ds(pl.multiple_of(n * 256, 256), 256)
        total = nn(oht[:, own], d_proj[:, cols])
        total = total + nt(low_q[...], w[0, cols, :])
        total = total + nt(low_k[...], w[1, cols, :])
        total = total + nt(low_v[...], w[2, cols, :])
        near_sums[:, cols] = total.astype(BF16)


def kernel(
    phonemes, durations, weights, d_out, coarse_in, fine_in, d_phon, d_weights, *scratch
):
    (
        w, cotan, coarse, fine, dur_own, dur_all, dur_rows, bounds, near, x, xt, oht, q, k, v, kt, vt,
        bias, p, att_t, d_proj, dq_t, dk, dv, ds, sums_landed, load_sems, dur_sems, near_sems, sum_sems, *rest
    ) = scratch
    out_refs, qkv_refs = rest[: len(rest) // 2], rest[len(rest) // 2 :]
    d_att = cotan
    at = place()
    seq = at["seq"]

    greet(at)
    tables = [
        pltpu.make_async_copy(coarse_in, coarse, load_sems.at[5]),
        pltpu.make_async_copy(fine_in, fine, load_sems.at[6]),
        pltpu.make_async_copy(
            phonemes.at[0], near.at[pl.ds(2 * P_DEV, P_DEV)], load_sems.at[7]
        ),
    ]
    loads = [pltpu.make_async_copy(weights.at[m], w.at[m], load_sems.at[m]) for m in range(4)]
    loads.append(pltpu.make_async_copy(d_out.at[0], cotan, load_sems.at[4]))
    for load in tables + loads[:3]:
        load.start()

    dur_own[...] = jnp.zeros_like(dur_own)
    dur_own[0:1, 0:P_DEV] = durations[...]
    dur_all[seq] = dur_own[...]
    near[NEAR:, :] = jnp.zeros((NEAR_PAD - NEAR, D), BF16)
    await_greetings()

    @pl.loop(1, SEQ)
    def _(steps):
        duration_copy(at, dur_own, dur_all, dur_sems, steps).start()

    for i in range(4):
        near_copy(at, phonemes, near, near_sems, i).start()
    for load in loads[3:]:
        load.start()
    make_bias(seq, bias)

    others = dur_all.at[pl.ds(0, SEQ - 1)]
    pltpu.make_async_copy(others, others, dur_sems.at[1]).wait()
    make_bounds(seq, dur_all, dur_rows, bounds)
    for i in range(4):
        near_copy(at, phonemes, near, near_sems, i).wait_recv()
    for load in tables:
        load.wait()

    make_inputs(seq, near, bounds, coarse, fine, x, xt, oht)
    for m in range(3):
        loads[m].wait()
    make_projections(x, w, q, k, v, kt, vt)
    forward_attention(q, k, vt, bias, p, att_t)
    loads[3].wait()
    loads[4].wait()
    output_backward(x, att_t, cotan, w, d_proj)

    out_turn = reduction_of(at, out_refs, (0, 1, 2, 0))
    turns = [
        reduction_of(at, [ref.at[g] for ref in qkv_refs], (0, 1, 2)) for g in range(GROUPS)
    ]

    def put_out(m, total):
        cols = m * COLS
        d_weights[3, :, cols : cols + 128] = total[:8]
        d_weights[3, :, cols + 128 : cols + COLS] = total[8:]

    def put_of(g):
        def put(m, total):
            cols = g * COLS
            d_weights[m, :, cols : cols + 128] = total[:8]
            d_weights[m, :, cols + 128 : cols + COLS] = total[8:]

        return put

    def out_grads():
        for j in range(GROUPS):
            cols = pl.ds(j * COLS, COLS)

            def store(core, y, value):
                out_refs[0][core, j, y] = value

            weight_grad(lambda rows: nn(att_t[rows, :], d_proj[:, cols]), store)

    def group_grads(g):
        cols = pl.ds(g * COLS, COLS)
        own = pl.ds(HALF, F_DEV)
        products = [
            lambda rows: nt(xt[rows, own], dq_t[cols, :]),
            lambda rows: nn(xt[rows, :], dk[:, cols]),
            lambda rows: nn(xt[rows, :], dv[:, cols]),
        ]
        for m in range(3):

            def store(core, y, value):
                qkv_refs[0][g, core, m, y] = value

            weight_grad(products[m], store)

    def both_phases(pair):
        if pair + 1 < PAIRS:
            score_grads(pair + 1, v, d_att, p, ds)
        pair_grads(pair, q, kt, d_att, p, ds, dq_t, dk, dv)

    out_grads()
    out_turn.send_core()
    attended_grads(w, d_proj, d_att)

    score_grads(0, v, d_att, p, ds)
    both_phases(0)
    both_phases(1)
    group_grads(0)
    turns[0].send_core()
    out_turn.first_sum()

    both_phases(2)
    both_phases(3)
    group_grads(1)
    turns[1].send_core()
    turns[0].first_sum()

    both_phases(4)
    both_phases(5)
    group_grads(2)
    turns[2].send_core()
    turns[1].first_sum()
    out_turn.next_sum(1)

    both_phases(6)
    both_phases(7)
    group_grads(3)
    turns[3].send_core()
    turns[2].first_sum()
    turns[0].next_sum(1)

    near_sums = near
    low_q, low_k, low_v = [x.at[pl.ds(m * NEAR_PAD, NEAR_PAD)] for m in range(3)]
    phoneme_low(oht, dq_t, dk, dv, low_q, low_k, low_v)
    turns[3].first_sum()
    turns[1].next_sum(1)
    out_turn.next_sum(2)
    phoneme_sums(oht, d_proj, w, low_q, low_k, low_v, near_sums)
    for i in range(4):
        sum_copy(at, near_sums, sums_landed, sum_sems, i).start()
    turns[2].next_sum(1)
    turns[0].next_sum(2)
    turns[3].next_sum(1)
    turns[1].next_sum(2)
    out_turn.last_sum(put_out)
    turns[2].next_sum(2)
    turns[0].last_sum(put_of(0))
    turns[3].next_sum(2)
    turns[1].last_sum(put_of(1))
    turns[2].last_sum(put_of(2))
    total = near_sums[2 * P_DEV : 3 * P_DEV, :].astype(F32)
    for i in range(4):
        sum_copy(at, near_sums, sums_landed, sum_sems, i).wait_recv()
        total = total + sums_landed[i].astype(F32)
    d_phon[0] = total.astype(BF16)
    turns[3].last_sum(put_of(3))

    pltpu.make_async_copy(others, others, dur_sems.at[0]).wait()
    for i in range(4):
        near_copy(at, phonemes, near, near_sems, i).wait_send()
        sum_copy(at, near_sums, sums_landed, sum_sems, i).wait_send()
    out_turn.drain()
    for turn in turns:
        turn.drain()


def on_device(phonemes, durations, weights, d_out):
    coarse, fine = position_tables()
    vmem = pl.BlockSpec(memory_space=pltpu.VMEM)
    hbm = pl.BlockSpec(memory_space=pl.ANY)
    scratch = [
        pltpu.VMEM((4, D, D), BF16),
        pltpu.VMEM((F_DEV, D), BF16),
        pltpu.VMEM(coarse.shape, F32),
        pltpu.VMEM(fine.shape, F32),
        pltpu.VMEM((8, 128), jnp.int32),
        pltpu.VMEM((SEQ, 8, 128), jnp.int32),
        pltpu.VMEM((8, 128), jnp.int32),
        pltpu.VMEM((8, NEAR_PAD), jnp.int32),
        pltpu.VMEM((NEAR_PAD, D), BF16),
        pltpu.VMEM((EXT, D), BF16),
        pltpu.VMEM((D, EXT), BF16),
        pltpu.VMEM((NEAR_PAD, EXT), BF16),
        pltpu.VMEM((F_DEV, D), BF16),
        pltpu.VMEM((EXT, D), BF16),
        pltpu.VMEM((EXT, D), BF16),
        pltpu.VMEM((D, EXT), BF16),
        pltpu.VMEM((D, EXT), BF16),
        pltpu.VMEM((TILES, SPAN, 2 * TILE), F32),
        pltpu.VMEM((PAIRS * TILES, SPAN, 2 * TILE), BF16),
        pltpu.VMEM((D, F_DEV), BF16),
        pltpu.VMEM((F_DEV, D), BF16),
        pltpu.VMEM((D, F_DEV), BF16),
        pltpu.VMEM((EXT, D), BF16),
        pltpu.VMEM((EXT, D), BF16),
        pltpu.VMEM((2, TILES, SPAN, 2 * TILE), BF16),
        pltpu.VMEM((4, P_DEV, D), BF16),
        pltpu.SemaphoreType.DMA((8,)),
        pltpu.SemaphoreType.DMA((2,)),
        pltpu.SemaphoreType.DMA((2, 4)),
        pltpu.SemaphoreType.DMA((2, 4)),
    ]
    scratch += reduction_scratch((), 4)
    scratch += reduction_scratch((GROUPS,), 3)
    return pl.pallas_call(
        kernel,
        out_shape=(
            jax.ShapeDtypeStruct((1, P_DEV, D), BF16),
            jax.ShapeDtypeStruct((4, 8, D), F32),
        ),
        in_specs=[hbm, vmem, hbm, hbm, hbm, hbm],
        out_specs=(vmem, vmem),
        scratch_shapes=scratch,
        compiler_params=pltpu.CompilerParams(
            collective_id=0, has_side_effects=True, vmem_limit_bytes=62 * 1024 * 1024
        ),
    )(phonemes, durations, weights, d_out, coarse, fine)


def solution(mesh):
    return jax.shard_map(
        on_device,
        mesh=mesh,
        in_specs=(P("grp", "seq", None), P("grp", "seq"), P(), P("grp", "seq", None)),
        out_specs=(P("grp", "seq", None), P(None, ("grp", "seq"), None)),
        check_vma=False,
    )
```

```python
import functools
import math

import jax
import jax.numpy as jnp
import numpy as np
from jax import lax
from jax.experimental import pallas as pl
from jax.experimental.pallas import tpu as pltpu
from jax.sharding import PartitionSpec as P

MESH = pl.DeviceIdType.MESH
BF16 = jnp.bfloat16
F32 = jnp.float32

D = 1024
HEADS = 16
WINDOW = 512
HALF = WINDOW // 2
F_DEV = 384
P_DEV = 48
SEQ = 32
GRP = 4
FRAMES = SEQ * F_DEV
EXT = F_DEV + WINDOW
TILE = 128
SPAN = TILE + WINDOW
TILES = F_DEV // TILE
PAIRS = HEADS // 2
NEAR = 5 * P_DEV
NEAR_PAD = 256
GROUPS = 4
COLS = D // GROUPS
GRAD_SCALE = 1.0 / math.sqrt(GRP * FRAMES)


def nn(a, b):
    return lax.dot_general(a, b, (((1,), (0,)), ((), ())), preferred_element_type=F32)


def nt(a, b):
    return lax.dot_general(a, b, (((1,), (1,)), ((), ())), preferred_element_type=F32)


def position_tables():
    half = D // 2
    rates = np.exp(np.arange(half) * (-math.log(10000.0) / half))
    tiles = SEQ * TILES + 2 * (HALF // TILE)
    coarse = (np.arange(tiles)[:, None] * TILE - HALF) * rates[None, :]
    fine = np.arange(TILE)[:, None] * rates[None, :]
    coarse = np.concatenate([np.sin(coarse), np.cos(coarse)], axis=1)
    fine = np.concatenate([np.sin(fine), np.cos(fine)], axis=1)
    pad = -coarse.shape[0] % 8
    coarse = np.pad(coarse, ((0, pad), (0, 0)))
    return coarse.astype(np.float32), fine.astype(np.float32)


def make_inputs(seq, near, bounds, coarse, fine, x, xt, oht):
    half = D // 2
    begins = bounds[0:1, :]
    ends = bounds[1:2, :]

    @pl.loop(0, EXT // TILE)
    def _(i):
        rows = pl.ds(pl.multiple_of(i * TILE, TILE), TILE)
        frame = lax.broadcasted_iota(jnp.int32, (TILE, NEAR_PAD), 0) + (seq * F_DEV - HALF + i * TILE)
        onehot = jnp.where((frame >= begins) & (frame < ends), 1.0, 0.0)
        onehot_low = onehot.astype(BF16)
        oht[:, rows] = onehot_low.T
        expanded = nn(onehot_low, near[...])
        base = coarse[pl.ds(seq * TILES + i, 1), :]
        sin_a, cos_a = base[:, :half], base[:, half:]
        sin_b, cos_b = fine[:, :half], fine[:, half:]
        x[rows, :half] = (expanded[:, :half] + (sin_a * cos_b + cos_a * sin_b)).astype(BF16)
        x[rows, half:] = (expanded[:, half:] + (cos_a * cos_b - sin_a * sin_b)).astype(BF16)

    for i in range(EXT // TILE):
        rows = pl.ds(i * TILE, TILE)
        xt[:, rows] = x[rows, :].T


def project_queries(n, x, w, q):
    cols = pl.ds(pl.multiple_of(n * 256, 256), 256)
    q[:, cols] = (nn(x[HALF : HALF + F_DEV, :], w[0, :, cols]).astype(BF16) * 0.125).astype(BF16)


def project_extended(n, x, weight, out, out_t):
    cols = pl.ds(pl.multiple_of(n * 256, 256), 256)
    rows = nn(x[...], weight[:, cols]).astype(BF16)
    out[:, cols] = rows
    out_t[cols, :] = rows.T


def make_bias(seq, bias):
    for i in range(TILES):
        key = lax.broadcasted_iota(jnp.int32, (SPAN, 2 * TILE), 0)
        query = lax.broadcasted_iota(jnp.int32, (SPAN, 2 * TILE), 1) % TILE
        frame = key + (seq * F_DEV - HALF + i * TILE)
        allowed = (key >= query) & (key < query + WINDOW) & (frame >= 0) & (frame < FRAMES)
        bias[i] = jnp.where(allowed, 0.0, -jnp.inf)


def two_heads(rows):
    lane = lax.broadcasted_iota(jnp.int32, rows.shape, 1)
    zero = jnp.zeros_like(rows)
    first = jnp.where(lane < 64, rows, zero)
    second = jnp.where(lane < 64, zero, rows)
    return jnp.concatenate([first, second], axis=0)


def own_halves(both):
    return jnp.concatenate([both[:64, :TILE], both[64:, TILE:]], axis=0)


def forward_attention(x, w, q, k, v, kt, vt, bias, p, att_t):
    def make_probs(pair, i):
        cols = pl.ds(pl.multiple_of(pair * 128, 128), 128)
        span = pl.ds(i * TILE, SPAN)
        rows = pl.ds(i * TILE, TILE)
        scores = nt(k[span, cols], two_heads(q[rows, cols])) + bias[i]
        peak = jnp.max(scores, axis=0, keepdims=True)
        raised = jnp.exp(scores - peak)
        total = jnp.sum(raised, axis=0, keepdims=True)
        p[pair * TILES + i] = (raised * (1.0 / total)).astype(BF16)

    def attend(pair, i):
        cols = pl.ds(pl.multiple_of(pair * 128, 128), 128)
        span = pl.ds(i * TILE, SPAN)
        rows = pl.ds(i * TILE, TILE)
        att_t[cols, rows] = own_halves(nn(vt[cols, span], p[pair * TILES + i])).astype(BF16)

    def project(n, i):
        if i == 0:
            project_queries(n, x, w, q)
        elif i == 1:
            project_extended(n, x, w.at[1], k, kt)
        else:
            project_extended(n, x, w.at[2], v, vt)

    def make_pair(pair):
        for i in range(TILES):
            make_probs(pair, i)

    def attend_pair(pair):
        for i in range(TILES):
            attend(pair, i)

    def project_group(n):
        for i in range(3):
            project(n, i)

    project_group(0)
    make_pair(0)
    project_group(1)
    attend_pair(0)
    make_pair(1)

    @pl.loop(1, GROUPS - 1)
    def _(g):
        attend_pair(2 * g - 1)
        make_pair(2 * g)
        project_group(g + 1)
        attend_pair(2 * g)
        make_pair(2 * g + 1)

    for pair in (PAIRS - 2, PAIRS - 1):
        attend_pair(pair - 1)
        make_pair(pair)
    attend_pair(PAIRS - 1)


def output_backward(x, att_t, d_out, w, d_proj):
    for i in range(TILES):
        rows = pl.ds(i * TILE, TILE)
        att = att_t[:, rows].T
        resid = x[HALF + i * TILE : HALF + (i + 1) * TILE, :].astype(F32) + nn(att, w[3])
        mean = jnp.mean(resid, axis=1, keepdims=True)
        centered = resid - mean
        inv_std = lax.rsqrt(jnp.mean(centered * centered, axis=1, keepdims=True) + 1e-5)
        normed = centered * inv_std
        cotan = d_out[rows, :].astype(F32)
        d_resid = inv_std * (
            cotan
            - jnp.mean(cotan, axis=1, keepdims=True)
            - normed * jnp.mean(cotan * normed, axis=1, keepdims=True)
        )
        d_proj[rows, :] = d_resid.astype(BF16)


def attended_grads(w, d_proj, d_att):
    @pl.loop(0, D // 256)
    def _(n):
        cols = pl.ds(pl.multiple_of(n * 256, 256), 256)
        d_att[:, cols] = nt(d_proj[...], w[3, cols, :]).astype(BF16)


def score_grads(pair, v, d_att, p, ds):
    cols = pl.ds(pair * 128, 128)
    for i in range(TILES):
        both_g = two_heads(d_att[i * TILE : (i + 1) * TILE, cols])
        d_probs = nt(v[pl.ds(i * TILE, SPAN), cols], both_g)
        probs = p[pair * TILES + i].astype(F32)
        weighted = probs * d_probs
        delta = jnp.sum(weighted, axis=0, keepdims=True)
        ds[pair % 2, i] = (weighted - probs * delta).astype(BF16)


def key_sums(cells, rights, put):
    first, second, third = rights
    middle = jnp.concatenate([cells(0, 256, 640), cells(1, 128, 512), cells(2, 0, 384)], axis=1)
    put(256, nn(middle, jnp.concatenate([first, second, third], axis=0)))
    put(0, nn(cells(0, 0, 128), first))
    near = jnp.concatenate([cells(0, 128, 256), cells(1, 0, 128)], axis=1)
    put(128, nn(near, jnp.concatenate([first, second], axis=0)))
    far = jnp.concatenate([cells(1, 512, 640), cells(2, 384, 512)], axis=1)
    put(640, nn(far, jnp.concatenate([second, third], axis=0)))
    put(768, nn(cells(2, 512, 640), third))


def pair_grads(pair, q, kt, d_att, p, ds, dq_t, dk, dv):
    cols = pl.ds(pair * 128, 128)
    tiles = [pl.ds(i * TILE, TILE) for i in range(TILES)]

    def put_keys(row, value):
        dk[pl.ds(row, value.shape[0]), cols] = value.astype(BF16)

    def put_values(row, value):
        dv[pl.ds(row, value.shape[0]), cols] = value.astype(BF16)

    for i in range(TILES):
        both = nn(kt[cols, pl.ds(i * TILE, SPAN)], ds[pair % 2, i])
        dq_t[cols, tiles[i]] = (own_halves(both) * 0.125).astype(BF16)
    key_sums(
        lambda i, begin, end: ds[pair % 2, i, begin:end, :],
        [two_heads(q[rows, cols]) for rows in tiles],
        put_keys,
    )
    key_sums(
        lambda i, begin, end: p[pair * TILES + i, begin:end, :],
        [two_heads(d_att[rows, cols]) for rows in tiles],
        put_values,
    )


def blocks_of(product):
    count = product.shape[0] // 8
    cells = product.reshape(count, 8, COLS)
    return jnp.concatenate([cells[:, :, :128], cells[:, :, 128:]], axis=1).astype(BF16)


def split_cores(blocks):
    pairs = blocks.reshape(blocks.shape[0] // 2, 2, 16, 128)
    return pairs[:, 0], pairs[:, 1]


def weight_grad(product_of, store):
    for t in range(D // 256):
        first, second = split_cores(blocks_of(product_of(pl.ds(t * 256, 256))))
        store(0, t, first.reshape(4, 4, 16, 128))
        store(1, t, second.reshape(4, 4, 16, 128))


AXES = ("y", "x", "z")
ROTATIONS = (("z", "x", "y"), ("x", "y", "z"), ("y", "z", "x"))


def place():
    y = lax.axis_index("grp")
    seq = lax.axis_index("seq")
    return {"y": y, "x": seq // 8, "z": (seq // 2) % 4, "core": seq % 2, "seq": seq}


def device_of(at):
    return (at["y"], at["x"] * 8 + at["z"] * 2 + at["core"])


def along(at, axis, steps):
    moved = dict(at)
    moved[axis] = (at[axis] + steps) % 4
    return moved


def at_axis(ref, dims, axis, index):
    where = tuple(index if dim == axis else slice(None) for dim in dims)
    return ref.at[where]


class Reduction:
    def __init__(self, at, parts, from_core, sums, landed, core_sems, send_sems, recv_sems, turns):
        self.at, self.parts, self.from_core = at, parts, from_core
        self.sums, self.landed = (parts.at[at["core"]],) + sums, landed
        self.core_sems, self.send_sems, self.recv_sems = core_sems, send_sems, recv_sems
        self.turns = turns

    def core_copy(self):
        sibling = dict(self.at)
        sibling["core"] = 1 - self.at["core"]
        return pltpu.make_async_remote_copy(
            src_ref=self.parts.at[sibling["core"]],
            dst_ref=self.from_core,
            send_sem=self.core_sems.at[0],
            recv_sem=self.core_sems.at[1],
            device_id=device_of(sibling),
            device_id_type=MESH,
        )

    def axis_copy(self, stage, m, steps):
        order = ROTATIONS[self.turns[m]]
        axis = order[stage]
        dims = [dim for dim in AXES if dim not in order[:stage]]
        target = along(self.at, axis, steps)
        return pltpu.make_async_remote_copy(
            src_ref=at_axis(self.sums[stage].at[m], dims, axis, target[axis]),
            dst_ref=self.landed[stage].at[steps - 1, m],
            send_sem=self.send_sems.at[stage],
            recv_sem=self.recv_sems.at[stage],
            device_id=device_of(target),
            device_id_type=MESH,
        )

    def send_core(self):
        self.core_copy().start()

    def send_axis(self, stage):
        for m in range(len(self.turns)):
            for steps in (2, 1, 3):
                self.axis_copy(stage, m, steps).start()

    def first_sum(self):
        self.core_copy().wait_recv()
        for m in range(len(self.turns)):
            for y in range(4):
                total = self.sums[0][m, y].astype(F32) + self.from_core[m, y].astype(F32)
                self.sums[0][m, y] = total.astype(BF16)
        self.send_axis(0)

    def axis_total(self, stage, m):
        order = ROTATIONS[self.turns[m]]
        axis = order[stage]
        dims = [dim for dim in AXES if dim not in order[:stage]]
        total = at_axis(self.sums[stage].at[m], dims, axis, self.at[axis])[...].astype(F32)
        for steps in (1, 2, 3):
            total = total + self.landed[stage][steps - 1, m].astype(F32)
        return total

    def await_axis(self, stage, sems):
        every = self.landed[stage]
        pltpu.make_async_copy(every, every, sems.at[stage]).wait()

    def next_sum(self, stage):
        self.await_axis(stage - 1, self.recv_sems)
        for m in range(len(self.turns)):
            self.sums[stage][m] = self.axis_total(stage - 1, m).astype(BF16)
        self.send_axis(stage)

    def last_sum(self, put):
        self.await_axis(2, self.recv_sems)
        for m in range(len(self.turns)):
            put(m, self.axis_total(2, m) * GRAD_SCALE)

    def drain(self):
        self.core_copy().wait_send()
        for stage in range(3):
            self.await_axis(stage, self.send_sems)


class PlaneReduction(Reduction):
    def plane_copies(self, m):
        order = ROTATIONS[self.turns[m]]
        first, second = [dim for dim in AXES if dim != order[0]]
        copies = []
        for steps in range(1, 16):
            target = along(along(self.at, first, steps // 4), second, steps % 4)
            copies.append(
                pltpu.make_async_remote_copy(
                    src_ref=self.sums[1].at[m, target[first], target[second]],
                    dst_ref=self.landed[1].at[steps, m],
                    send_sem=self.send_sems.at[1],
                    recv_sem=self.recv_sems.at[1],
                    device_id=device_of(target),
                    device_id_type=MESH,
                )
            )
        return copies

    def send_axis(self, stage):
        if stage == 0:
            super().send_axis(0)
            return
        for m in range(len(self.turns)):
            for copy in self.plane_copies(m):
                copy.start()

    def await_plane(self, sems):
        every = self.landed[1].at[pl.ds(1, 15)]
        pltpu.make_async_copy(every, every, sems.at[1]).wait()

    def last_sum(self, put):
        self.await_plane(self.recv_sems)
        for m in range(len(self.turns)):
            order = ROTATIONS[self.turns[m]]
            first, second = [dim for dim in AXES if dim != order[0]]
            total = self.sums[1][m, self.at[first], self.at[second]].astype(F32)
            for steps in range(1, 16):
                total = total + self.landed[1][steps, m].astype(F32)
            put(m, total * GRAD_SCALE)

    def drain(self):
        self.core_copy().wait_send()
        self.await_axis(0, self.send_sems)
        self.await_plane(self.send_sems)


def plane_scratch(n):
    return [
        pltpu.VMEM((2, n, 4, 4, 4, 16, 128), BF16),
        pltpu.VMEM((n, 4, 4, 4, 16, 128), BF16),
        pltpu.VMEM((n, 4, 4, 16, 128), BF16),
        pltpu.VMEM((3, n, 4, 4, 16, 128), BF16),
        pltpu.VMEM((16, n, 16, 128), BF16),
        pltpu.SemaphoreType.DMA((2,)),
        pltpu.SemaphoreType.DMA((2,)),
        pltpu.SemaphoreType.DMA((2,)),
    ]


def plane_of(at, refs, turns):
    parts, from_core, s1, l0, l1, core_sems, send_sems, recv_sems = refs
    return PlaneReduction(
        at, parts, from_core, (s1,), (l0, l1), core_sems, send_sems, recv_sems, turns
    )


def reduction_scratch(lead, n):
    return [
        pltpu.VMEM(lead + (2, n, 4, 4, 4, 16, 128), BF16),
        pltpu.VMEM(lead + (n, 4, 4, 4, 16, 128), BF16),
        pltpu.VMEM(lead + (n, 4, 4, 16, 128), BF16),
        pltpu.VMEM(lead + (n, 4, 16, 128), BF16),
        pltpu.VMEM(lead + (3, n, 4, 4, 16, 128), BF16),
        pltpu.VMEM(lead + (3, n, 4, 16, 128), BF16),
        pltpu.VMEM(lead + (3, n, 16, 128), BF16),
        pltpu.SemaphoreType.DMA(lead + (2,)),
        pltpu.SemaphoreType.DMA(lead + (3,)),
        pltpu.SemaphoreType.DMA(lead + (3,)),
    ]


def reduction_of(at, refs, turns):
    parts, from_core, s1, s2, l0, l1, l2, core_sems, send_sems, recv_sems = refs
    return Reduction(
        at, parts, from_core, (s1, s2), (l0, l1, l2), core_sems, send_sems, recv_sems, turns
    )


def greet(at):
    barrier = pltpu.get_barrier_semaphore()

    @pl.loop(1, SEQ)
    def _(steps):
        pl.semaphore_signal(
            barrier,
            inc=1,
            device_id=(at["y"], (at["seq"] + steps) % SEQ),
            device_id_type=MESH,
        )

    for steps in (1, 2, 3):
        pl.semaphore_signal(
            barrier, inc=1, device_id=device_of(along(at, "y", steps)), device_id_type=MESH
        )
        for axis in ("x", "z"):
            for others in (1, 2, 3):
                target = along(along(at, "y", steps), axis, others)
                pl.semaphore_signal(
                    barrier, inc=1, device_id=device_of(target), device_id_type=MESH
                )


def await_greetings():
    pl.semaphore_wait(pltpu.get_barrier_semaphore(), SEQ - 1 + 3 + 18)


NEAR_STEPS = (1, -1, 2, -2)


def near_copy(at, phonemes, near, sems, i):
    steps = NEAR_STEPS[i]
    return pltpu.make_async_remote_copy(
        src_ref=phonemes.at[0],
        dst_ref=near.at[pl.ds((2 - steps) * P_DEV, P_DEV)],
        send_sem=sems.at[0, i],
        recv_sem=sems.at[1, i],
        device_id=(at["y"], (at["seq"] + steps + SEQ) % SEQ),
        device_id_type=MESH,
    )


def duration_copy(at, own, all_durations, sems, steps):
    return pltpu.make_async_remote_copy(
        src_ref=own,
        dst_ref=all_durations.at[at["seq"]],
        send_sem=sems.at[0],
        recv_sem=sems.at[1],
        device_id=(at["y"], (at["seq"] + steps) % SEQ),
        device_id_type=MESH,
    )


def make_bounds(seq, all_durations, rows, bounds):
    everyone = all_durations[:, 0, :]
    block_of = lax.broadcasted_iota(jnp.int32, (SEQ, 128), 0)
    rows[...] = jnp.zeros_like(rows)
    before = []
    for i in range(5):
        index = (seq + i - 2 + SEQ) % SEQ
        rows[i : i + 1, :] = all_durations[index][0:1, :]
        earlier = jnp.sum(jnp.where(block_of < index, everyone, 0), axis=0, keepdims=True)
        before.append(jnp.sum(earlier, axis=1, keepdims=True))
    lane = lax.broadcasted_iota(jnp.int32, (8, 128), 1)
    lengths = rows[...]
    running = lengths
    for shift in (1, 2, 4, 8, 16, 32):
        running = running + jnp.where(lane >= shift, pltpu.roll(running, shift, 1), 0)
    valid = lane < P_DEV
    ends = jnp.where(valid, running, 0)
    begins = jnp.where(valid, running - lengths, 0)
    empty = jnp.zeros((8, 128), jnp.int32)
    all_ends = jnp.zeros((1, 256), jnp.int32)
    all_begins = jnp.zeros((1, 256), jnp.int32)
    wide = lax.broadcasted_iota(jnp.int32, (1, 256), 1)
    for i in range(5):
        here = (wide >= i * P_DEV) & (wide < (i + 1) * P_DEV)
        end_row = jnp.concatenate([ends, empty], axis=1)
        begin_row = jnp.concatenate([begins, empty], axis=1)
        if i:
            end_row = pltpu.roll(end_row, i * P_DEV, 1)
            begin_row = pltpu.roll(begin_row, i * P_DEV, 1)
        all_ends = jnp.where(here, end_row[i : i + 1] + before[i], all_ends)
        all_begins = jnp.where(here, begin_row[i : i + 1] + before[i], all_begins)
    bounds[0:1, :] = all_begins
    bounds[1:2, :] = all_ends


def sum_copy(at, near_sums, landed, sems, i):
    steps = NEAR_STEPS[i]
    return pltpu.make_async_remote_copy(
        src_ref=near_sums.at[pl.ds((2 + steps) * P_DEV, P_DEV)],
        dst_ref=landed.at[i],
        send_sem=sems.at[0, i],
        recv_sem=sems.at[1, i],
        device_id=(at["y"], (at["seq"] + steps + SEQ) % SEQ),
        device_id_type=MESH,
    )


def phoneme_low(oht, dq_t, dk, dv, low_q, low_k, low_v):
    own = pl.ds(HALF, F_DEV)

    @pl.loop(0, D // 256)
    def _(n):
        cols = pl.ds(pl.multiple_of(n * 256, 256), 256)
        low_q[:, cols] = nt(oht[:, own], dq_t[cols, :]).astype(BF16)
        low_k[:, cols] = nn(oht[...], dk[:, cols]).astype(BF16)
        low_v[:, cols] = nn(oht[...], dv[:, cols]).astype(BF16)


def phoneme_sums(oht, d_proj, w, low_q, low_k, low_v, near_sums):
    own = pl.ds(HALF, F_DEV)

    @pl.loop(0, D // 256)
    def _(n):
        cols = pl.ds(pl.multiple_of(n * 256, 256), 256)
        total = nn(oht[:, own], d_proj[:, cols])
        total = total + nt(low_q[...], w[0, cols, :])
        total = total + nt(low_k[...], w[1, cols, :])
        total = total + nt(low_v[...], w[2, cols, :])
        near_sums[:, cols] = total.astype(BF16)


def kernel(
    phonemes, durations, weights, d_out, coarse_in, fine_in, out_phon, out_weights, *scratch
):
    (
        d_phon, d_weights, lengths, w, cotan, coarse, fine, dur_own, dur_all, dur_rows, bounds, near, x, xt, oht, q, k, v, kt, vt,
        bias, p, att_t, d_proj, dq_t, dk, dv, ds, sums_landed, load_sems, dur_sems, near_sems, sum_sems, out_sems, *rest
    ) = scratch
    out_refs, qkv_refs, last_refs = rest[:10], rest[10:20], rest[20:]
    d_att = cotan
    at = place()
    seq = at["seq"]

    greet(at)
    load_lengths = pltpu.make_async_copy(durations, lengths, load_sems.at[8])
    load_lengths.start()
    tables = [
        pltpu.make_async_copy(coarse_in, coarse, load_sems.at[5]),
        pltpu.make_async_copy(fine_in, fine, load_sems.at[6]),
        pltpu.make_async_copy(
            phonemes.at[0], near.at[pl.ds(2 * P_DEV, P_DEV)], load_sems.at[7]
        ),
    ]
    loads = [pltpu.make_async_copy(weights.at[m], w.at[m], load_sems.at[m]) for m in range(4)]
    loads.append(pltpu.make_async_copy(d_out.at[0], cotan, load_sems.at[4]))
    for load in tables + loads[:3]:
        load.start()

    dur_own[...] = jnp.zeros_like(dur_own)
    load_lengths.wait()
    dur_own[0:1, 0:P_DEV] = lengths[...]
    dur_all[seq] = dur_own[...]
    near[NEAR:, :] = jnp.zeros((NEAR_PAD - NEAR, D), BF16)
    await_greetings()

    @pl.loop(1, SEQ)
    def _(steps):
        duration_copy(at, dur_own, dur_all, dur_sems, steps).start()

    for i in range(4):
        near_copy(at, phonemes, near, near_sems, i).start()
    for load in loads[3:]:
        load.start()
    make_bias(seq, bias)

    others = dur_all.at[pl.ds(0, SEQ - 1)]
    pltpu.make_async_copy(others, others, dur_sems.at[1]).wait()
    make_bounds(seq, dur_all, dur_rows, bounds)
    for i in range(4):
        near_copy(at, phonemes, near, near_sems, i).wait_recv()
    for load in tables:
        load.wait()

    make_inputs(seq, near, bounds, coarse, fine, x, xt, oht)
    for m in range(3):
        loads[m].wait()
    forward_attention(x, w, q, k, v, kt, vt, bias, p, att_t)
    loads[3].wait()
    loads[4].wait()
    output_backward(x, att_t, cotan, w, d_proj)

    out_turn = reduction_of(at, out_refs, (0, 1, 2, 0))
    turns = [
        reduction_of(at, [ref.at[g] for ref in qkv_refs], (0, 1, 2)) for g in range(GROUPS - 1)
    ]
    turns.append(plane_of(at, last_refs, (0, 1, 2)))

    def put_out(m, total):
        cols = m * COLS
        d_weights[3, :, cols : cols + 128] = total[:8]
        d_weights[3, :, cols + 128 : cols + COLS] = total[8:]

    def put_of(g):
        def put(m, total):
            cols = g * COLS
            d_weights[m, :, cols : cols + 128] = total[:8]
            d_weights[m, :, cols + 128 : cols + COLS] = total[8:]

        return put

    def out_grads():
        for j in range(GROUPS):
            cols = pl.ds(j * COLS, COLS)

            def store(core, y, value):
                out_refs[0][core, j, y] = value

            weight_grad(lambda rows: nn(att_t[rows, :], d_proj[:, cols]), store)

    def group_grads(g):
        cols = pl.ds(g * COLS, COLS)
        own = pl.ds(HALF, F_DEV)
        products = [
            lambda rows: nt(xt[rows, own], dq_t[cols, :]),
            lambda rows: nn(xt[rows, :], dk[:, cols]),
            lambda rows: nn(xt[rows, :], dv[:, cols]),
        ]
        for m in range(3):

            def store(core, y, value):
                turns[g].parts[core, m, y] = value

            weight_grad(products[m], store)

    def both_phases(pair):
        if pair + 1 < PAIRS:
            score_grads(pair + 1, v, d_att, p, ds)
        pair_grads(pair, q, kt, d_att, p, ds, dq_t, dk, dv)

    out_grads()
    out_turn.send_core()
    attended_grads(w, d_proj, d_att)

    score_grads(0, v, d_att, p, ds)
    both_phases(0)
    both_phases(1)
    group_grads(0)
    turns[0].send_core()
    out_turn.first_sum()

    both_phases(2)
    both_phases(3)
    group_grads(1)
    turns[1].send_core()
    turns[0].first_sum()

    both_phases(4)
    both_phases(5)
    group_grads(2)
    turns[2].send_core()
    turns[1].first_sum()
    out_turn.next_sum(1)

    both_phases(6)
    both_phases(7)
    group_grads(3)
    turns[3].send_core()
    turns[2].first_sum()
    turns[0].next_sum(1)

    outputs = [
        pltpu.make_async_copy(d_phon, out_phon.at[0], out_sems.at[0]),
        pltpu.make_async_copy(d_weights.at[3], out_weights.at[3], out_sems.at[1]),
        pltpu.make_async_copy(
            d_weights.at[pl.ds(0, 3)], out_weights.at[pl.ds(0, 3)], out_sems.at[2]
        ),
    ]
    near_sums = near
    low_q, low_k, low_v = [x.at[pl.ds(m * NEAR_PAD, NEAR_PAD)] for m in range(3)]
    phoneme_low(oht, dq_t, dk, dv, low_q, low_k, low_v)
    turns[3].first_sum()
    turns[1].next_sum(1)
    out_turn.next_sum(2)
    phoneme_sums(oht, d_proj, w, low_q, low_k, low_v, near_sums)
    for i in range(4):
        sum_copy(at, near_sums, sums_landed, sum_sems, i).start()
    turns[2].next_sum(1)
    turns[0].next_sum(2)
    turns[3].next_sum(1)
    turns[1].next_sum(2)
    out_turn.last_sum(put_out)
    outputs[1].start()
    turns[2].next_sum(2)
    turns[0].last_sum(put_of(0))
    turns[1].last_sum(put_of(1))
    turns[2].last_sum(put_of(2))
    total = near_sums[2 * P_DEV : 3 * P_DEV, :].astype(F32)
    for i in range(4):
        sum_copy(at, near_sums, sums_landed, sum_sems, i).wait_recv()
        total = total + sums_landed[i].astype(F32)
    d_phon[...] = total.astype(BF16)
    outputs[0].start()
    turns[3].last_sum(put_of(3))
    outputs[2].start()

    pltpu.make_async_copy(others, others, dur_sems.at[0]).wait()
    for i in range(4):
        near_copy(at, phonemes, near, near_sems, i).wait_send()
        sum_copy(at, near_sums, sums_landed, sum_sems, i).wait_send()
    out_turn.drain()
    for turn in turns:
        turn.drain()
    for copy in outputs:
        copy.wait()


def on_device(phonemes, durations, weights, d_out):
    coarse, fine = position_tables()
    hbm = pl.BlockSpec(memory_space=pl.ANY)
    scratch = [
        pltpu.VMEM((P_DEV, D), BF16),
        pltpu.VMEM((4, 8, D), F32),
        pltpu.VMEM((1, P_DEV), jnp.int32),
        pltpu.VMEM((4, D, D), BF16),
        pltpu.VMEM((F_DEV, D), BF16),
        pltpu.VMEM(coarse.shape, F32),
        pltpu.VMEM(fine.shape, F32),
        pltpu.VMEM((8, 128), jnp.int32),
        pltpu.VMEM((SEQ, 8, 128), jnp.int32),
        pltpu.VMEM((8, 128), jnp.int32),
        pltpu.VMEM((8, NEAR_PAD), jnp.int32),
        pltpu.VMEM((NEAR_PAD, D), BF16),
        pltpu.VMEM((EXT, D), BF16),
        pltpu.VMEM((D, EXT), BF16),
        pltpu.VMEM((NEAR_PAD, EXT), BF16),
        pltpu.VMEM((F_DEV, D), BF16),
        pltpu.VMEM((EXT, D), BF16),
        pltpu.VMEM((EXT, D), BF16),
        pltpu.VMEM((D, EXT), BF16),
        pltpu.VMEM((D, EXT), BF16),
        pltpu.VMEM((TILES, SPAN, 2 * TILE), F32),
        pltpu.VMEM((PAIRS * TILES, SPAN, 2 * TILE), BF16),
        pltpu.VMEM((D, F_DEV), BF16),
        pltpu.VMEM((F_DEV, D), BF16),
        pltpu.VMEM((D, F_DEV), BF16),
        pltpu.VMEM((EXT, D), BF16),
        pltpu.VMEM((EXT, D), BF16),
        pltpu.VMEM((2, TILES, SPAN, 2 * TILE), BF16),
        pltpu.VMEM((4, P_DEV, D), BF16),
        pltpu.SemaphoreType.DMA((9,)),
        pltpu.SemaphoreType.DMA((2,)),
        pltpu.SemaphoreType.DMA((2, 4)),
        pltpu.SemaphoreType.DMA((2, 4)),
        pltpu.SemaphoreType.DMA((3,)),
    ]
    scratch += reduction_scratch((), 4)
    scratch += reduction_scratch((GROUPS - 1,), 3)
    scratch += plane_scratch(3)
    return pl.pallas_call(
        kernel,
        out_shape=(
            jax.ShapeDtypeStruct((1, P_DEV, D), BF16),
            jax.ShapeDtypeStruct((4, 8, D), F32),
        ),
        in_specs=[hbm] * 6,
        out_specs=(hbm, hbm),
        scratch_shapes=scratch,
        compiler_params=pltpu.CompilerParams(
            collective_id=0, has_side_effects=True, vmem_limit_bytes=62 * 1024 * 1024
        ),
    )(phonemes, durations, weights, d_out, coarse, fine)


def solution(mesh):
    return jax.shard_map(
        on_device,
        mesh=mesh,
        in_specs=(P("grp", "seq", None), P("grp", "seq"), P(), P("grp", "seq", None)),
        out_specs=(P("grp", "seq", None), P(None, ("grp", "seq"), None)),
        check_vma=False,
    )
```

```python
import functools
import math

import jax
import jax.numpy as jnp
import numpy as np
from jax import lax
from jax.experimental import pallas as pl
from jax.experimental.pallas import tpu as pltpu
from jax.sharding import PartitionSpec as P

MESH = pl.DeviceIdType.MESH
BF16 = jnp.bfloat16
F32 = jnp.float32

D = 1024
HEADS = 16
WINDOW = 512
HALF = WINDOW // 2
F_DEV = 384
P_DEV = 48
SEQ = 32
GRP = 4
FRAMES = SEQ * F_DEV
EXT = F_DEV + WINDOW
TILE = 128
SPAN = TILE + WINDOW
TILES = F_DEV // TILE
PAIRS = HEADS // 2
NEAR = 5 * P_DEV
NEAR_PAD = 256
GROUPS = 4
COLS = D // GROUPS
GRAD_SCALE = 1.0 / math.sqrt(GRP * FRAMES)


def nn(a, b):
    return lax.dot_general(a, b, (((1,), (0,)), ((), ())), preferred_element_type=F32)


def nt(a, b):
    return lax.dot_general(a, b, (((1,), (1,)), ((), ())), preferred_element_type=F32)


def position_tables():
    half = D // 2
    rates = np.exp(np.arange(half) * (-math.log(10000.0) / half))
    tiles = SEQ * TILES + 2 * (HALF // TILE)
    coarse = (np.arange(tiles)[:, None] * TILE - HALF) * rates[None, :]
    fine = np.arange(TILE)[:, None] * rates[None, :]
    coarse = np.concatenate([np.sin(coarse), np.cos(coarse)], axis=1)
    fine = np.concatenate([np.sin(fine), np.cos(fine)], axis=1)
    pad = -coarse.shape[0] % 8
    coarse = np.pad(coarse, ((0, pad), (0, 0)))
    return coarse.astype(np.float32), fine.astype(np.float32)


def make_inputs(seq, near, bounds, coarse, fine, x, xt, oht):
    half = D // 2
    begins = bounds[0:1, :]
    ends = bounds[1:2, :]

    @pl.loop(0, EXT // TILE)
    def _(i):
        rows = pl.ds(pl.multiple_of(i * TILE, TILE), TILE)
        frame = lax.broadcasted_iota(jnp.int32, (TILE, NEAR_PAD), 0) + (seq * F_DEV - HALF + i * TILE)
        onehot = jnp.where((frame >= begins) & (frame < ends), 1.0, 0.0)
        onehot_low = onehot.astype(BF16)
        oht[:, rows] = onehot_low.T
        expanded = nn(onehot_low, near[...])
        base = coarse[pl.ds(seq * TILES + i, 1), :]
        sin_a, cos_a = base[:, :half], base[:, half:]
        sin_b, cos_b = fine[:, :half], fine[:, half:]
        x[rows, :half] = (expanded[:, :half] + (sin_a * cos_b + cos_a * sin_b)).astype(BF16)
        x[rows, half:] = (expanded[:, half:] + (cos_a * cos_b - sin_a * sin_b)).astype(BF16)

    for i in range(EXT // TILE):
        rows = pl.ds(i * TILE, TILE)
        xt[:, rows] = x[rows, :].T


def project_queries(n, x, w, q):
    cols = pl.ds(pl.multiple_of(n * 256, 256), 256)
    q[:, cols] = (nn(x[HALF : HALF + F_DEV, :], w[0, :, cols]).astype(BF16) * 0.125).astype(BF16)


def project_extended(n, x, weight, out, out_t):
    cols = pl.ds(pl.multiple_of(n * 256, 256), 256)
    rows = nn(x[...], weight[:, cols]).astype(BF16)
    out[:, cols] = rows
    out_t[cols, :] = rows.T


def make_bias(seq, bias):
    for i in range(TILES):
        key = lax.broadcasted_iota(jnp.int32, (SPAN, 2 * TILE), 0)
        query = lax.broadcasted_iota(jnp.int32, (SPAN, 2 * TILE), 1) % TILE
        frame = key + (seq * F_DEV - HALF + i * TILE)
        allowed = (key >= query) & (key < query + WINDOW) & (frame >= 0) & (frame < FRAMES)
        bias[i] = jnp.where(allowed, 0.0, -jnp.inf)


def two_heads(rows):
    lane = lax.broadcasted_iota(jnp.int32, rows.shape, 1)
    zero = jnp.zeros_like(rows)
    first = jnp.where(lane < 64, rows, zero)
    second = jnp.where(lane < 64, zero, rows)
    return jnp.concatenate([first, second], axis=0)


def own_halves(both):
    return jnp.concatenate([both[:64, :TILE], both[64:, TILE:]], axis=0)


def forward_attention(x, w, q, k, v, kt, vt, bias, p, att_t):
    def make_probs(pair, i):
        cols = pl.ds(pl.multiple_of(pair * 128, 128), 128)
        span = pl.ds(i * TILE, SPAN)
        rows = pl.ds(i * TILE, TILE)
        scores = nt(k[span, cols], two_heads(q[rows, cols])) + bias[i]
        peak = jnp.max(scores, axis=0, keepdims=True)
        raised = jnp.exp(scores - peak)
        total = jnp.sum(raised, axis=0, keepdims=True)
        p[pair * TILES + i] = (raised * (1.0 / total)).astype(BF16)

    def attend(pair, i):
        cols = pl.ds(pl.multiple_of(pair * 128, 128), 128)
        span = pl.ds(i * TILE, SPAN)
        rows = pl.ds(i * TILE, TILE)
        att_t[cols, rows] = own_halves(nn(vt[cols, span], p[pair * TILES + i])).astype(BF16)

    def project(n, i):
        if i == 0:
            project_queries(n, x, w, q)
        elif i == 1:
            project_extended(n, x, w.at[1], k, kt)
        else:
            project_extended(n, x, w.at[2], v, vt)

    def make_pair(pair):
        for i in range(TILES):
            make_probs(pair, i)

    def attend_pair(pair):
        for i in range(TILES):
            attend(pair, i)

    def project_group(n):
        for i in range(3):
            project(n, i)

    project_group(0)
    make_pair(0)
    project_group(1)
    attend_pair(0)
    make_pair(1)

    @pl.loop(1, GROUPS - 1)
    def _(g):
        attend_pair(2 * g - 1)
        make_pair(2 * g)
        project_group(g + 1)
        attend_pair(2 * g)
        make_pair(2 * g + 1)

    for pair in (PAIRS - 2, PAIRS - 1):
        attend_pair(pair - 1)
        make_pair(pair)
    attend_pair(PAIRS - 1)


def output_backward(x, att_t, d_out, w, d_proj):
    for i in range(TILES):
        rows = pl.ds(i * TILE, TILE)
        att = att_t[:, rows].T
        resid = x[HALF + i * TILE : HALF + (i + 1) * TILE, :].astype(F32) + nn(att, w[3])
        mean = jnp.mean(resid, axis=1, keepdims=True)
        centered = resid - mean
        inv_std = lax.rsqrt(jnp.mean(centered * centered, axis=1, keepdims=True) + 1e-5)
        normed = centered * inv_std
        cotan = d_out[rows, :].astype(F32)
        d_resid = inv_std * (
            cotan
            - jnp.mean(cotan, axis=1, keepdims=True)
            - normed * jnp.mean(cotan * normed, axis=1, keepdims=True)
        )
        d_proj[rows, :] = d_resid.astype(BF16)


def attended_grads(w, d_proj, d_att):
    @pl.loop(0, D // 256)
    def _(n):
        cols = pl.ds(pl.multiple_of(n * 256, 256), 256)
        d_att[:, cols] = nt(d_proj[...], w[3, cols, :]).astype(BF16)


def score_grads(pair, v, d_att, p, ds):
    cols = pl.ds(pair * 128, 128)
    for i in range(TILES):
        both_g = two_heads(d_att[i * TILE : (i + 1) * TILE, cols])
        d_probs = nt(v[pl.ds(i * TILE, SPAN), cols], both_g)
        probs = p[pair * TILES + i].astype(F32)
        weighted = probs * d_probs
        delta = jnp.sum(weighted, axis=0, keepdims=True)
        ds[pair % 2, i] = (weighted - probs * delta).astype(BF16)


def key_sums(cells, rights, put):
    first, second, third = rights
    middle = jnp.concatenate([cells(0, 256, 640), cells(1, 128, 512), cells(2, 0, 384)], axis=1)
    put(256, nn(middle, jnp.concatenate([first, second, third], axis=0)))
    put(0, nn(cells(0, 0, 128), first))
    near = jnp.concatenate([cells(0, 128, 256), cells(1, 0, 128)], axis=1)
    put(128, nn(near, jnp.concatenate([first, second], axis=0)))
    far = jnp.concatenate([cells(1, 512, 640), cells(2, 384, 512)], axis=1)
    put(640, nn(far, jnp.concatenate([second, third], axis=0)))
    put(768, nn(cells(2, 512, 640), third))


def pair_grads(pair, q, kt, d_att, p, ds, dq_t, dk, dv):
    cols = pl.ds(pair * 128, 128)
    tiles = [pl.ds(i * TILE, TILE) for i in range(TILES)]

    def put_keys(row, value):
        dk[pl.ds(row, value.shape[0]), cols] = value.astype(BF16)

    def put_values(row, value):
        dv[pl.ds(row, value.shape[0]), cols] = value.astype(BF16)

    for i in range(TILES):
        both = nn(kt[cols, pl.ds(i * TILE, SPAN)], ds[pair % 2, i])
        dq_t[cols, tiles[i]] = (own_halves(both) * 0.125).astype(BF16)
    key_sums(
        lambda i, begin, end: ds[pair % 2, i, begin:end, :],
        [two_heads(q[rows, cols]) for rows in tiles],
        put_keys,
    )
    key_sums(
        lambda i, begin, end: p[pair * TILES + i, begin:end, :],
        [two_heads(d_att[rows, cols]) for rows in tiles],
        put_values,
    )


def blocks_of(product):
    count = product.shape[0] // 8
    cells = product.reshape(count, 8, COLS)
    return jnp.concatenate([cells[:, :, :128], cells[:, :, 128:]], axis=1).astype(BF16)


def split_cores(blocks):
    pairs = blocks.reshape(blocks.shape[0] // 2, 2, 16, 128)
    return pairs[:, 0], pairs[:, 1]


def weight_grad(product_of, store):
    for t in range(D // 256):
        first, second = split_cores(blocks_of(product_of(pl.ds(t * 256, 256))))
        store(0, t, first.reshape(4, 4, 16, 128))
        store(1, t, second.reshape(4, 4, 16, 128))


AXES = ("y", "x", "z")
ROTATIONS = (("z", "x", "y"), ("x", "y", "z"), ("y", "z", "x"))


def place():
    y = lax.axis_index("grp")
    seq = lax.axis_index("seq")
    return {"y": y, "x": seq // 8, "z": (seq // 2) % 4, "core": seq % 2, "seq": seq}


def device_of(at):
    return (at["y"], at["x"] * 8 + at["z"] * 2 + at["core"])


def along(at, axis, steps):
    moved = dict(at)
    moved[axis] = (at[axis] + steps) % 4
    return moved


def at_axis(ref, dims, axis, index):
    where = tuple(index if dim == axis else slice(None) for dim in dims)
    return ref.at[where]


class Reduction:
    def __init__(self, at, parts, from_core, sums, landed, core_sems, send_sems, recv_sems, turns):
        self.at, self.parts, self.from_core = at, parts, from_core
        self.sums, self.landed = (parts.at[at["core"]],) + sums, landed
        self.core_sems, self.send_sems, self.recv_sems = core_sems, send_sems, recv_sems
        self.turns = turns

    def core_copy(self, m):
        sibling = dict(self.at)
        sibling["core"] = 1 - self.at["core"]
        return pltpu.make_async_remote_copy(
            src_ref=self.parts.at[sibling["core"], m],
            dst_ref=self.from_core.at[m],
            send_sem=self.core_sems.at[0],
            recv_sem=self.core_sems.at[1],
            device_id=device_of(sibling),
            device_id_type=MESH,
        )

    def axis_copy(self, stage, m, steps):
        order = ROTATIONS[self.turns[m]]
        axis = order[stage]
        dims = [dim for dim in AXES if dim not in order[:stage]]
        target = along(self.at, axis, steps)
        return pltpu.make_async_remote_copy(
            src_ref=at_axis(self.sums[stage].at[m], dims, axis, target[axis]),
            dst_ref=self.landed[stage].at[steps - 1, m],
            send_sem=self.send_sems.at[stage],
            recv_sem=self.recv_sems.at[stage],
            device_id=device_of(target),
            device_id_type=MESH,
        )

    def send_core(self, m):
        self.core_copy(m).start()

    def await_core(self, side):
        pltpu.make_async_copy(self.from_core, self.from_core, self.core_sems.at[side]).wait()

    def send_axis(self, stage):
        for m in range(len(self.turns)):
            for steps in (2, 1, 3):
                self.axis_copy(stage, m, steps).start()

    def first_sum(self):
        self.await_core(1)
        for m in range(len(self.turns)):
            for y in range(4):
                self.sums[0][m, y] = self.sums[0][m, y] + self.from_core[m, y]
        self.send_axis(0)

    def axis_total(self, stage, m):
        order = ROTATIONS[self.turns[m]]
        axis = order[stage]
        dims = [dim for dim in AXES if dim not in order[:stage]]
        total = at_axis(self.sums[stage].at[m], dims, axis, self.at[axis])[...].astype(F32)
        for steps in (1, 2, 3):
            total = total + self.landed[stage][steps - 1, m].astype(F32)
        return total

    def await_axis(self, stage, sems):
        every = self.landed[stage]
        pltpu.make_async_copy(every, every, sems.at[stage]).wait()

    def next_sum(self, stage):
        self.await_axis(stage - 1, self.recv_sems)
        for m in range(len(self.turns)):
            self.sums[stage][m] = self.axis_total(stage - 1, m).astype(BF16)
        self.send_axis(stage)

    def last_sum(self, put):
        self.await_axis(2, self.recv_sems)
        for m in range(len(self.turns)):
            put(m, self.axis_total(2, m) * GRAD_SCALE)

    def drain(self):
        self.await_core(0)
        for stage in range(3):
            self.await_axis(stage, self.send_sems)


class PlaneReduction(Reduction):
    def plane_copies(self, m):
        order = ROTATIONS[self.turns[m]]
        first, second = [dim for dim in AXES if dim != order[0]]
        copies = []
        for steps in range(1, 16):
            target = along(along(self.at, first, steps // 4), second, steps % 4)
            copies.append(
                pltpu.make_async_remote_copy(
                    src_ref=self.sums[1].at[m, target[first], target[second]],
                    dst_ref=self.landed[1].at[steps, m],
                    send_sem=self.send_sems.at[1],
                    recv_sem=self.recv_sems.at[1],
                    device_id=device_of(target),
                    device_id_type=MESH,
                )
            )
        return copies

    def send_axis(self, stage):
        if stage == 0:
            super().send_axis(0)
            return
        for m in range(len(self.turns)):
            for copy in self.plane_copies(m):
                copy.start()

    def await_plane(self, sems):
        every = self.landed[1].at[pl.ds(1, 15)]
        pltpu.make_async_copy(every, every, sems.at[1]).wait()

    def last_sum(self, put):
        self.await_plane(self.recv_sems)
        for m in range(len(self.turns)):
            order = ROTATIONS[self.turns[m]]
            first, second = [dim for dim in AXES if dim != order[0]]
            total = self.sums[1][m, self.at[first], self.at[second]].astype(F32)
            for steps in range(1, 16):
                total = total + self.landed[1][steps, m].astype(F32)
            put(m, total * GRAD_SCALE)

    def drain(self):
        self.await_core(0)
        self.await_axis(0, self.send_sems)
        self.await_plane(self.send_sems)


def plane_scratch(n):
    return [
        pltpu.VMEM((2, n, 4, 4, 4, 16, 128), BF16),
        pltpu.VMEM((n, 4, 4, 4, 16, 128), BF16),
        pltpu.VMEM((n, 4, 4, 16, 128), BF16),
        pltpu.VMEM((3, n, 4, 4, 16, 128), BF16),
        pltpu.VMEM((16, n, 16, 128), BF16),
        pltpu.SemaphoreType.DMA((2,)),
        pltpu.SemaphoreType.DMA((2,)),
        pltpu.SemaphoreType.DMA((2,)),
    ]


def plane_of(at, refs, turns):
    parts, from_core, s1, l0, l1, core_sems, send_sems, recv_sems = refs
    return PlaneReduction(
        at, parts, from_core, (s1,), (l0, l1), core_sems, send_sems, recv_sems, turns
    )


def reduction_scratch(lead, n):
    return [
        pltpu.VMEM(lead + (2, n, 4, 4, 4, 16, 128), BF16),
        pltpu.VMEM(lead + (n, 4, 4, 4, 16, 128), BF16),
        pltpu.VMEM(lead + (n, 4, 4, 16, 128), BF16),
        pltpu.VMEM(lead + (n, 4, 16, 128), BF16),
        pltpu.VMEM(lead + (3, n, 4, 4, 16, 128), BF16),
        pltpu.VMEM(lead + (3, n, 4, 16, 128), BF16),
        pltpu.VMEM(lead + (3, n, 16, 128), BF16),
        pltpu.SemaphoreType.DMA(lead + (2,)),
        pltpu.SemaphoreType.DMA(lead + (3,)),
        pltpu.SemaphoreType.DMA(lead + (3,)),
    ]


def reduction_of(at, refs, turns):
    parts, from_core, s1, s2, l0, l1, l2, core_sems, send_sems, recv_sems = refs
    return Reduction(
        at, parts, from_core, (s1, s2), (l0, l1, l2), core_sems, send_sems, recv_sems, turns
    )


def greet(at):
    barrier = pltpu.get_barrier_semaphore()

    @pl.loop(1, SEQ)
    def _(steps):
        pl.semaphore_signal(
            barrier,
            inc=1,
            device_id=(at["y"], (at["seq"] + steps) % SEQ),
            device_id_type=MESH,
        )

    for steps in (1, 2, 3):
        pl.semaphore_signal(
            barrier, inc=1, device_id=device_of(along(at, "y", steps)), device_id_type=MESH
        )
        for axis in ("x", "z"):
            for others in (1, 2, 3):
                target = along(along(at, "y", steps), axis, others)
                pl.semaphore_signal(
                    barrier, inc=1, device_id=device_of(target), device_id_type=MESH
                )


def await_greetings():
    pl.semaphore_wait(pltpu.get_barrier_semaphore(), SEQ - 1 + 3 + 18)


NEAR_STEPS = (1, -1, 2, -2)


def near_copy(at, phonemes, near, sems, i):
    steps = NEAR_STEPS[i]
    return pltpu.make_async_remote_copy(
        src_ref=phonemes.at[0],
        dst_ref=near.at[pl.ds((2 - steps) * P_DEV, P_DEV)],
        send_sem=sems.at[0, i],
        recv_sem=sems.at[1, i],
        device_id=(at["y"], (at["seq"] + steps + SEQ) % SEQ),
        device_id_type=MESH,
    )


def duration_copy(at, own, all_durations, sems, steps):
    return pltpu.make_async_remote_copy(
        src_ref=own,
        dst_ref=all_durations.at[at["seq"]],
        send_sem=sems.at[0],
        recv_sem=sems.at[1],
        device_id=(at["y"], (at["seq"] + steps) % SEQ),
        device_id_type=MESH,
    )


def make_bounds(seq, all_durations, rows, bounds):
    everyone = all_durations[:, 0, :]
    block_of = lax.broadcasted_iota(jnp.int32, (SEQ, 128), 0)
    rows[...] = jnp.zeros_like(rows)
    before = []
    for i in range(5):
        index = (seq + i - 2 + SEQ) % SEQ
        rows[i : i + 1, :] = all_durations[index][0:1, :]
        earlier = jnp.sum(jnp.where(block_of < index, everyone, 0), axis=0, keepdims=True)
        before.append(jnp.sum(earlier, axis=1, keepdims=True))
    lane = lax.broadcasted_iota(jnp.int32, (8, 128), 1)
    lengths = rows[...]
    running = lengths
    for shift in (1, 2, 4, 8, 16, 32):
        running = running + jnp.where(lane >= shift, pltpu.roll(running, shift, 1), 0)
    valid = lane < P_DEV
    ends = jnp.where(valid, running, 0)
    begins = jnp.where(valid, running - lengths, 0)
    empty = jnp.zeros((8, 128), jnp.int32)
    all_ends = jnp.zeros((1, 256), jnp.int32)
    all_begins = jnp.zeros((1, 256), jnp.int32)
    wide = lax.broadcasted_iota(jnp.int32, (1, 256), 1)
    for i in range(5):
        here = (wide >= i * P_DEV) & (wide < (i + 1) * P_DEV)
        end_row = jnp.concatenate([ends, empty], axis=1)
        begin_row = jnp.concatenate([begins, empty], axis=1)
        if i:
            end_row = pltpu.roll(end_row, i * P_DEV, 1)
            begin_row = pltpu.roll(begin_row, i * P_DEV, 1)
        all_ends = jnp.where(here, end_row[i : i + 1] + before[i], all_ends)
        all_begins = jnp.where(here, begin_row[i : i + 1] + before[i], all_begins)
    bounds[0:1, :] = all_begins
    bounds[1:2, :] = all_ends


def sum_copy(at, near_sums, landed, sems, i):
    steps = NEAR_STEPS[i]
    return pltpu.make_async_remote_copy(
        src_ref=near_sums.at[pl.ds((2 + steps) * P_DEV, P_DEV)],
        dst_ref=landed.at[i],
        send_sem=sems.at[0, i],
        recv_sem=sems.at[1, i],
        device_id=(at["y"], (at["seq"] + steps + SEQ) % SEQ),
        device_id_type=MESH,
    )


def phoneme_low(oht, dq_t, dk, dv, low_q, low_k, low_v):
    own = pl.ds(HALF, F_DEV)

    @pl.loop(0, D // 256)
    def _(n):
        cols = pl.ds(pl.multiple_of(n * 256, 256), 256)
        low_q[:, cols] = nt(oht[:, own], dq_t[cols, :]).astype(BF16)
        low_k[:, cols] = nn(oht[...], dk[:, cols]).astype(BF16)
        low_v[:, cols] = nn(oht[...], dv[:, cols]).astype(BF16)


def phoneme_sums(oht, d_proj, w, low_q, low_k, low_v, near_sums):
    own = pl.ds(HALF, F_DEV)

    @pl.loop(0, D // 256)
    def _(n):
        cols = pl.ds(pl.multiple_of(n * 256, 256), 256)
        total = nn(oht[:, own], d_proj[:, cols])
        total = total + nt(low_q[...], w[0, cols, :])
        total = total + nt(low_k[...], w[1, cols, :])
        total = total + nt(low_v[...], w[2, cols, :])
        near_sums[:, cols] = total.astype(BF16)


def kernel(
    phonemes, durations, weights, d_out, coarse_in, fine_in, out_phon, out_weights, *scratch
):
    (
        d_phon, d_weights, lengths, w, cotan, coarse, fine, dur_own, dur_all, dur_rows, bounds, near, x, xt, oht, q, k, v, kt, vt,
        bias, p, att_t, d_proj, dq_t, dk, dv, ds, sums_landed, load_sems, dur_sems, near_sems, sum_sems, out_sems, *rest
    ) = scratch
    out_refs, qkv_refs, last_refs = rest[:10], rest[10:20], rest[20:]
    d_att = cotan
    at = place()
    seq = at["seq"]

    greet(at)
    load_lengths = pltpu.make_async_copy(durations, lengths, load_sems.at[8])
    load_lengths.start()
    tables = [
        pltpu.make_async_copy(coarse_in, coarse, load_sems.at[5]),
        pltpu.make_async_copy(fine_in, fine, load_sems.at[6]),
        pltpu.make_async_copy(
            phonemes.at[0], near.at[pl.ds(2 * P_DEV, P_DEV)], load_sems.at[7]
        ),
    ]
    loads = [pltpu.make_async_copy(weights.at[m], w.at[m], load_sems.at[m]) for m in range(4)]
    loads.append(pltpu.make_async_copy(d_out.at[0], cotan, load_sems.at[4]))
    for load in tables + loads[:3]:
        load.start()

    dur_own[...] = jnp.zeros_like(dur_own)
    load_lengths.wait()
    dur_own[0:1, 0:P_DEV] = lengths[...]
    dur_all[seq] = dur_own[...]
    near[NEAR:, :] = jnp.zeros((NEAR_PAD - NEAR, D), BF16)
    await_greetings()

    @pl.loop(1, SEQ)
    def _(steps):
        duration_copy(at, dur_own, dur_all, dur_sems, steps).start()

    for i in range(4):
        near_copy(at, phonemes, near, near_sems, i).start()
    for load in loads[3:]:
        load.start()
    make_bias(seq, bias)

    others = dur_all.at[pl.ds(0, SEQ - 1)]
    pltpu.make_async_copy(others, others, dur_sems.at[1]).wait()
    make_bounds(seq, dur_all, dur_rows, bounds)
    for i in range(4):
        near_copy(at, phonemes, near, near_sems, i).wait_recv()
    for load in tables:
        load.wait()

    make_inputs(seq, near, bounds, coarse, fine, x, xt, oht)
    for m in range(3):
        loads[m].wait()
    forward_attention(x, w, q, k, v, kt, vt, bias, p, att_t)
    loads[3].wait()
    loads[4].wait()
    output_backward(x, att_t, cotan, w, d_proj)

    out_turn = reduction_of(at, out_refs, (0, 1, 2, 0))
    turns = [
        reduction_of(at, [ref.at[g] for ref in qkv_refs], (0, 1, 2)) for g in range(GROUPS - 1)
    ]
    turns.append(plane_of(at, last_refs, (0, 1, 2)))

    def put_out(m, total):
        cols = m * COLS
        d_weights[3, :, cols : cols + 128] = total[:8]
        d_weights[3, :, cols + 128 : cols + COLS] = total[8:]

    def put_of(g):
        def put(m, total):
            cols = g * COLS
            d_weights[m, :, cols : cols + 128] = total[:8]
            d_weights[m, :, cols + 128 : cols + COLS] = total[8:]

        return put

    def out_grads():
        for j in range(GROUPS):
            cols = pl.ds(j * COLS, COLS)

            def store(core, y, value):
                out_refs[0][core, j, y] = value

            weight_grad(lambda rows: nn(att_t[rows, :], d_proj[:, cols]), store)
            out_turn.send_core(j)

    def group_grads(g):
        cols = pl.ds(g * COLS, COLS)
        own = pl.ds(HALF, F_DEV)
        products = [
            lambda rows: nt(xt[rows, own], dq_t[cols, :]),
            lambda rows: nn(xt[rows, :], dk[:, cols]),
            lambda rows: nn(xt[rows, :], dv[:, cols]),
        ]
        for m in range(3):

            def store(core, y, value):
                turns[g].parts[core, m, y] = value

            weight_grad(products[m], store)
            turns[g].send_core(m)

    def both_phases(pair):
        if pair + 1 < PAIRS:
            score_grads(pair + 1, v, d_att, p, ds)
        pair_grads(pair, q, kt, d_att, p, ds, dq_t, dk, dv)

    out_grads()
    attended_grads(w, d_proj, d_att)

    score_grads(0, v, d_att, p, ds)
    both_phases(0)
    both_phases(1)
    group_grads(0)
    out_turn.first_sum()

    both_phases(2)
    both_phases(3)
    group_grads(1)
    turns[0].first_sum()

    both_phases(4)
    both_phases(5)
    group_grads(2)
    turns[1].first_sum()
    out_turn.next_sum(1)

    both_phases(6)
    turns[2].first_sum()
    both_phases(7)
    group_grads(3)
    turns[0].next_sum(1)

    outputs = [
        pltpu.make_async_copy(d_phon, out_phon.at[0], out_sems.at[0]),
        pltpu.make_async_copy(d_weights.at[3], out_weights.at[3], out_sems.at[1]),
        pltpu.make_async_copy(
            d_weights.at[pl.ds(0, 3)], out_weights.at[pl.ds(0, 3)], out_sems.at[2]
        ),
    ]
    near_sums = near
    low_q, low_k, low_v = [x.at[pl.ds(m * NEAR_PAD, NEAR_PAD)] for m in range(3)]
    turns[3].first_sum()
    out_turn.next_sum(2)
    turns[1].next_sum(1)
    phoneme_low(oht, dq_t, dk, dv, low_q, low_k, low_v)
    turns[2].next_sum(1)
    phoneme_sums(oht, d_proj, w, low_q, low_k, low_v, near_sums)
    for i in range(4):
        sum_copy(at, near_sums, sums_landed, sum_sems, i).start()
    turns[3].next_sum(1)
    turns[0].next_sum(2)
    turns[1].next_sum(2)
    turns[2].next_sum(2)
    out_turn.last_sum(put_out)
    outputs[1].start()
    turns[0].last_sum(put_of(0))
    turns[1].last_sum(put_of(1))
    turns[2].last_sum(put_of(2))
    total = near_sums[2 * P_DEV : 3 * P_DEV, :].astype(F32)
    for i in range(4):
        sum_copy(at, near_sums, sums_landed, sum_sems, i).wait_recv()
        total = total + sums_landed[i].astype(F32)
    d_phon[...] = total.astype(BF16)
    outputs[0].start()
    turns[3].last_sum(put_of(3))
    outputs[2].start()

    pltpu.make_async_copy(others, others, dur_sems.at[0]).wait()
    for i in range(4):
        near_copy(at, phonemes, near, near_sems, i).wait_send()
        sum_copy(at, near_sums, sums_landed, sum_sems, i).wait_send()
    out_turn.drain()
    for turn in turns:
        turn.drain()
    for copy in outputs:
        copy.wait()


def on_device(phonemes, durations, weights, d_out):
    coarse, fine = position_tables()
    hbm = pl.BlockSpec(memory_space=pl.ANY)
    scratch = [
        pltpu.VMEM((P_DEV, D), BF16),
        pltpu.VMEM((4, 8, D), F32),
        pltpu.VMEM((1, P_DEV), jnp.int32),
        pltpu.VMEM((4, D, D), BF16),
        pltpu.VMEM((F_DEV, D), BF16),
        pltpu.VMEM(coarse.shape, F32),
        pltpu.VMEM(fine.shape, F32),
        pltpu.VMEM((8, 128), jnp.int32),
        pltpu.VMEM((SEQ, 8, 128), jnp.int32),
        pltpu.VMEM((8, 128), jnp.int32),
        pltpu.VMEM((8, NEAR_PAD), jnp.int32),
        pltpu.VMEM((NEAR_PAD, D), BF16),
        pltpu.VMEM((EXT, D), BF16),
        pltpu.VMEM((D, EXT), BF16),
        pltpu.VMEM((NEAR_PAD, EXT), BF16),
        pltpu.VMEM((F_DEV, D), BF16),
        pltpu.VMEM((EXT, D), BF16),
        pltpu.VMEM((EXT, D), BF16),
        pltpu.VMEM((D, EXT), BF16),
        pltpu.VMEM((D, EXT), BF16),
        pltpu.VMEM((TILES, SPAN, 2 * TILE), F32),
        pltpu.VMEM((PAIRS * TILES, SPAN, 2 * TILE), BF16),
        pltpu.VMEM((D, F_DEV), BF16),
        pltpu.VMEM((F_DEV, D), BF16),
        pltpu.VMEM((D, F_DEV), BF16),
        pltpu.VMEM((EXT, D), BF16),
        pltpu.VMEM((EXT, D), BF16),
        pltpu.VMEM((2, TILES, SPAN, 2 * TILE), BF16),
        pltpu.VMEM((4, P_DEV, D), BF16),
        pltpu.SemaphoreType.DMA((9,)),
        pltpu.SemaphoreType.DMA((2,)),
        pltpu.SemaphoreType.DMA((2, 4)),
        pltpu.SemaphoreType.DMA((2, 4)),
        pltpu.SemaphoreType.DMA((3,)),
    ]
    scratch += reduction_scratch((), 4)
    scratch += reduction_scratch((GROUPS - 1,), 3)
    scratch += plane_scratch(3)
    return pl.pallas_call(
        kernel,
        out_shape=(
            jax.ShapeDtypeStruct((1, P_DEV, D), BF16),
            jax.ShapeDtypeStruct((4, 8, D), F32),
        ),
        in_specs=[hbm] * 6,
        out_specs=(hbm, hbm),
        scratch_shapes=scratch,
        compiler_params=pltpu.CompilerParams(
            collective_id=0, has_side_effects=True, vmem_limit_bytes=62 * 1024 * 1024
        ),
    )(phonemes, durations, weights, d_out, coarse, fine)


def solution(mesh):
    return jax.shard_map(
        on_device,
        mesh=mesh,
        in_specs=(P("grp", "seq", None), P("grp", "seq"), P(), P("grp", "seq", None)),
        out_specs=(P("grp", "seq", None), P(None, ("grp", "seq"), None)),
        check_vma=False,
    )
```
